32 devices in a mesh: alpha: 8 (over z, core), beta: 4 (over y, x).
Axes of the slice: x: 2, y: 2, z: 4, core: 2. Of those that a mesh axis runs over, the one named last changes fastest.
Arguments:
- start_vector: float32 [256, 98304], P('alpha', 'beta'), may hold values from -6 to 6
- precondition: float32 [256, 98304], P('alpha', 'beta'), may hold values from 1 to 10
- alpha_hamiltonian: float32 [256, 256], replicated, may hold values from -0.375 to 0.375
- alpha_pairs: float32 [2, 256, 256], replicated, may hold values from -0.375 to 0.375
- pair_tables: float32 [4, 128, 128], replicated, may hold values from -0.375 to 0.375
- source_blocks: int32 [768, 2], P('beta'), may hold values from 0 to 767
- pair_index: int32 [768, 2], P('beta'), may hold values from 0 to 3
- phase_signs: int32 [768, 2], P('beta'), may hold values from -1 to 1, as said below
- cross_pairs: int32 [2, 768], P(None, 'beta'), may hold values from 0 to 3
- cross_signs: int32 [2, 768], P(None, 'beta'), may hold values from -1 to 1, as said below
Outputs:
- correction: float32 [256, 98304], P('alpha', 'beta')
- sigma_next: float32 [256, 98304], P('alpha', 'beta')
The draws below stay inside these ranges and needn't reach their ends.
Inputs may be any that keep to these rules, and one draw needn't show every extreme that they name: `phase_signs`: each entry is -1 or 1. `cross_signs`: each entry is -1 or 1.
All inputs are finite; a program needn't handle non-finite values.
Results may differ from the reference program's by a relative error of at most 0.000076.
Values sent between devices are 32-bit elements; how exact they have to be, the bound alone decides.
No kernel may reach another device: no remote copies, remote signals or barrier semaphores. Data moves between devices by JAX's collectives and lax.ppermute only.
A program may use at most 256 MiB of HBM per device.

```python
import math
import jax
import jax.numpy as jnp
from jax import lax

NA_DEV = 32
NB = 98304
SB = 128
KB = 2
NPAIR = 4
Q = 2
NA = 256
NBLK = 768


def draw_phase_signs(key, part):
    key = jax.random.fold_in(key, 11)
    return (2 * jax.random.randint(key, (NBLK, KB), 0, 2) - 1).astype(jnp.int32)


def draw_cross_signs(key, part):
    key = jax.random.fold_in(key, 23)
    return (2 * jax.random.randint(key, (Q, NBLK), 0, 2) - 1).astype(jnp.int32)


def touch_ends(entries, stream_key, low, top_value):
    shape = entries.shape
    place = [jax.random.randint(jax.random.fold_in(stream_key, axis), (), 0, shape[axis]) for axis in range(len(shape))]
    entries = entries.at[tuple(place)].set(low)
    longest = shape.index(max(shape))
    place[longest] = (place[longest] + 1) % shape[longest]
    return entries.at[tuple(place)].set(top_value)


def block_scale(rng, dims, cuts, least, top_value):
    gain = 1.0
    for axis_at, parts in cuts:
        heights = jax.random.uniform(jax.random.fold_in(jax.random.fold_in(rng, 6), axis_at), (parts,), jnp.float32, least / len(cuts), top_value / len(cuts))
        gain = gain * jnp.repeat(jnp.exp(heights), dims[axis_at] // parts).reshape((-1,) + (1,) * (len(dims) - 1 - axis_at))
    return gain


def bell_draw(own_key, dims, deviation, limit, split=(), held_as=jnp.bfloat16):
    drawn = deviation * jax.random.normal(own_key, dims, jnp.float32)
    if split:
        drawn = drawn * block_scale(own_key, dims, split, -0.22, 0.18)
    return jnp.clip(drawn, -limit, limit).astype(held_as)


def setup_inputs(seed: int = 0) -> dict:
    seeds = jax.random.split(jax.random.key(seed), 11)
    return {
        "start_vector": bell_draw(seeds[0], (NA, NB), 1.0, 6.0, ((0, 8), (1, 4)), jnp.float32),
        "precondition": jnp.clip(jnp.exp(math.log(10.0) - 2.3025851 * jax.random.uniform(seeds[1], (NA, NB), jnp.float32) ** block_scale(seeds[1], (NA, NB), ((0, 8), (1, 4)), -0.2, 0.2)), 1.0, 10.0),
        "alpha_hamiltonian": bell_draw(seeds[2], (NA, NA), NA ** -0.5, 0.375, (), jnp.float32),
        "alpha_pairs": bell_draw(seeds[3], (Q, NA, NA), NA ** -0.5, 0.375, (), jnp.float32),
        "pair_tables": bell_draw(seeds[4], (NPAIR, SB, SB), (SB * KB) ** -0.5, 0.375, (), jnp.float32),
        "source_blocks": touch_ends(jax.random.randint(seeds[5], (NBLK, KB), 0, NBLK), jax.random.fold_in(seeds[5], 1), 0, NBLK - 1).astype(jnp.int32),
        "pair_index": touch_ends(jax.random.randint(seeds[6], (NBLK, KB), 0, NPAIR), jax.random.fold_in(seeds[6], 1), 0, NPAIR - 1).astype(jnp.int32),
        "phase_signs": draw_phase_signs(jax.random.fold_in(seeds[10], 71), 0),
        "cross_pairs": touch_ends(jax.random.randint(seeds[8], (Q, NBLK), 0, NPAIR), jax.random.fold_in(seeds[8], 1), 0, NPAIR - 1).astype(jnp.int32),
        "cross_signs": draw_cross_signs(jax.random.fold_in(seeds[10], 71), 0),
    }


highest = lax.Precision.HIGHEST


def sigma_full(vector, alpha_hamiltonian, alpha_pairs, pair_tables, source_blocks, pair_index, phase_signs, cross_pairs, cross_signs):
    grouped = vector.reshape(NA // NA_DEV, NA_DEV, NBLK, SB)
    beta_tabs = pair_tables[pair_index] * phase_signs.astype(jnp.float32)[:, :, None, None]
    cross_tabs = pair_tables[cross_pairs] * cross_signs.astype(jnp.float32)[:, :, None, None]

    def row_group(group):
        picked = group[:, source_blocks]
        beta_term = jnp.einsum('rtkc,tkcd->rtd', picked, beta_tabs, precision=highest)
        crossed = jnp.einsum('rtc,qtcd->qrtd', group, cross_tabs, precision=highest)
        return beta_term, crossed

    beta_term, crossed = lax.map(row_group, grouped)
    beta_term = beta_term.reshape(NA, NB)
    crossed = jnp.transpose(crossed, (1, 0, 2, 3, 4)).reshape(Q, NA, NB)
    alpha_term = jnp.dot(alpha_hamiltonian, vector, precision=highest)
    alpha_term = alpha_term + jnp.einsum('qij,qjc->ic', alpha_pairs, crossed, precision=highest)
    return beta_term + alpha_term


def reference(start_vector, precondition, alpha_hamiltonian, alpha_pairs, pair_tables, source_blocks, pair_index, phase_signs, cross_pairs, cross_signs):
    tables = (alpha_hamiltonian, alpha_pairs, pair_tables, source_blocks, pair_index, phase_signs, cross_pairs, cross_signs)
    first = sigma_full(start_vector, *tables)
    theta = jnp.sum(start_vector * first) / jnp.sum(start_vector * start_vector)
    correction = (first - theta * start_vector) / precondition
    return correction, sigma_full(correction, *tables)
```

```python
import jax
import jax.numpy as jnp
from jax import lax
from jax.experimental import pallas as pl
from jax.experimental.pallas import tpu as pltpu
from jax.sharding import PartitionSpec as P

SB = 128
CHUNKS = 2
VMEM_BYTES = 48 * 1024 * 1024
f32 = jnp.float32
bf16 = jnp.bfloat16


def params():
    return pltpu.CompilerParams(vmem_limit_bytes=VMEM_BYTES)


def divisor(number, most):
    return max(d for d in range(1, most + 1) if number % d == 0)


def halves(x):
    high = x.astype(bf16)
    return high, (x - high.astype(f32)).astype(bf16)


def mul(a, b):
    return jnp.dot(a, b, preferred_element_type=f32)


def cost(flops, count):
    return pl.CostEstimate(flops=flops, bytes_accessed=count, transcendentals=0)


def pack(vector, place, chunk, n, width):
    rows = vector.shape[0]

    def kernel(place_ref, *refs):
        for source, target in zip(refs[: n - 1], refs[n - 1 :]):
            target[...] = source[...]

    def part(k):
        return lambda g, place: (0, chunk * n + lax.rem(place[0] + k, n))

    return pl.pallas_call(
        kernel,
        grid_spec=pltpu.PrefetchScalarGridSpec(
            num_scalar_prefetch=1,
            grid=(1,),
            in_specs=[pl.BlockSpec((rows, width), part(k)) for k in range(1, n)],
            out_specs=[pl.BlockSpec((rows, width), lambda g, place: (0, 0))] * (n - 1),
        ),
        out_shape=[jax.ShapeDtypeStruct((rows, width), f32)] * (n - 1),
        compiler_params=params(),
        cost_estimate=cost(0, 8 * (n - 1) * rows * width),
        name="pack",
    )(place, *[vector] * (n - 1))


def rotate(parts, n, back=False):
    moved = []
    for k, part in enumerate(parts, 1):
        pairs = [(i, ((i // 2 + k) % n) * 2 + i % 2) for i in range(2 * n)]
        moved.append(lax.ppermute(part, "alpha", pairs))
    return moved


def alpha_partial(own, own_chunk, received, couplings, pair_tables, cross_pairs, cross_signs, place, chunk, n, width):
    rows = own.shape[0]
    deep = n * rows
    out_rows, depth = couplings.shape
    npair = pair_tables.shape[0]
    nq = cross_pairs.shape[0]
    blocks = width // SB
    per = divisor(blocks, 4)
    steps = blocks // per
    wide = per * SB

    def kernel(place_ref, pairs_ref, signs_ref, *refs):
        sources = refs[:n]
        a_ref, t_ref, mine_ref, other_ref, a_twice, a_low, t_high, t_low, b = refs[n:]
        g = pl.program_id(0)
        z = place_ref[0]

        @pl.when(g == 0)
        def _():
            high, low = halves(a_ref[...])
            a_twice[:, :depth] = high
            a_twice[:, depth:] = high
            a_low[...] = low
            for p in range(npair):
                high, low = halves(t_ref[p])
                t_high[p] = high
                t_low[p] = low

        for k in range(n):
            high, low = halves(sources[k][...])
            start = pl.multiple_of(lax.rem(z + n - k, n) * rows, rows)
            b[pl.ds(start, rows), :] = high
            b[pl.ds(depth + start, rows), :] = low
        first = (chunk * n + z) * blocks + g * per
        for t in range(per):
            at = slice(t * SB, (t + 1) * SB)
            high = b[:deep, at]
            both = jnp.concatenate([high, b[depth : depth + deep, at]], axis=1)
            for q in range(nq):
                p = pairs_ref[q, first + t]
                table = t_high[p]
                x = mul(both, jnp.concatenate([table, table], axis=0)) + mul(high, t_low[p])
                x = x * signs_ref[q, first + t].astype(f32)
                x_high, x_low = halves(x)
                row = (q + 1) * deep
                b[row : row + deep, at] = x_high
                b[depth + row : depth + row + deep, at] = x_low
        total = mul(a_twice[...], b[...]) + mul(a_low[...], b[:depth, :])
        mine_ref[...] = total[:deep]
        other_ref[...] = total[deep:]

    if own_chunk is None:
        own_spec = pl.BlockSpec((rows, wide), lambda g, place, *_: (0, g))
    else:
        own_spec = pl.BlockSpec((rows, wide), lambda g, place, *_: (0, (own_chunk * n + place[0]) * steps + g))
    part_spec = pl.BlockSpec((rows, wide), lambda g, *_: (0, g))
    return pl.pallas_call(
        kernel,
        grid_spec=pltpu.PrefetchScalarGridSpec(
            num_scalar_prefetch=3,
            grid=(steps,),
            in_specs=[own_spec]
            + [part_spec] * (n - 1)
            + [
                pl.BlockSpec(couplings.shape, lambda g, *_: (0, 0)),
                pl.BlockSpec(pair_tables.shape, lambda g, *_: (0, 0, 0)),
            ],
            out_specs=[pl.BlockSpec((deep, wide), lambda g, *_: (0, g))] * 2,
            scratch_shapes=[
                pltpu.VMEM((out_rows, 2 * depth), bf16),
                pltpu.VMEM((out_rows, depth), bf16),
                pltpu.VMEM(pair_tables.shape, bf16),
                pltpu.VMEM(pair_tables.shape, bf16),
                pltpu.VMEM((2 * depth, wide), bf16),
            ],
        ),
        out_shape=[jax.ShapeDtypeStruct((deep, width), f32)] * 2,
        compiler_params=params(),
        cost_estimate=cost(6 * out_rows * depth * width, 4 * width * rows * n * 3),
        name="alpha_partial",
    )(place, cross_pairs, cross_signs, own, *received, couplings, pair_tables)


def join(mine, other, vectors, place, n, width, with_dot):
    deep = mine.shape[0]
    rows = deep // n
    blocks = width // SB
    steps = divisor(blocks, 4)
    wide = width // steps

    def kernel(place_ref, mine_ref, other_ref, *refs):
        v_refs = refs[: len(vectors)]
        outs = refs[len(vectors) : len(vectors) + n]
        z = place_ref[0]
        dot = jnp.zeros((rows, wide), f32)
        for k in range(n):
            at = pl.ds(pl.multiple_of(lax.rem(z + k, n) * rows, rows), rows)
            total = mine_ref[at, :] + other_ref[at, :]
            outs[k][...] = total
            if with_dot:
                dot = dot + total * v_refs[(n - k) % n][...]
        if with_dot:
            refs[-1][...] = jnp.sum(dot, axis=0, keepdims=True)

    def fixed(place):
        return (0, 0)

    part_spec = pl.BlockSpec((rows, wide), lambda g, place: (0, g))
    v_specs = [part_spec] * len(vectors)
    arrays = list(vectors)
    if with_dot:
        own, own_chunk = vectors[0]
        v_specs[0] = pl.BlockSpec((rows, wide), lambda g, place: (0, (own_chunk * n + place[0]) * steps + g))
        arrays[0] = own
    out = pl.pallas_call(
        kernel,
        grid_spec=pltpu.PrefetchScalarGridSpec(
            num_scalar_prefetch=1,
            grid=(steps,),
            in_specs=[pl.BlockSpec((deep, wide), lambda g, place: (0, g))] * 2 + v_specs,
            out_specs=[part_spec] * n + ([pl.BlockSpec((1, wide), lambda g, place: (0, g))] if with_dot else []),
        ),
        out_shape=[jax.ShapeDtypeStruct((rows, width), f32)] * n
        + ([jax.ShapeDtypeStruct((1, width), f32)] if with_dot else []),
        compiler_params=params(),
        cost_estimate=cost(2 * deep * width, 4 * 4 * deep * width),
        name="join",
    )(place, mine, other, *arrays)
    return out[:n], (jnp.sum(out[n]) if with_dot else None)


def gather_blocks(vector, lists):
    rows = vector.shape[0]
    count, cap = lists.shape

    def kernel(lists_ref, v_ref, *outs):
        for k in range(count):

            @pl.loop(0, cap, unroll=8)
            def _(j):
                at = pl.multiple_of(lists_ref[k, j] * SB, SB)
                outs[k][j] = v_ref[:, pl.ds(at, SB)]

    return pl.pallas_call(
        kernel,
        grid_spec=pltpu.PrefetchScalarGridSpec(
            num_scalar_prefetch=1,
            grid=(1,),
            in_specs=[pl.BlockSpec(vector.shape, lambda g, lists: (0, 0))],
            out_specs=[pl.BlockSpec((cap, rows, SB), lambda g, lists: (0, 0, 0))] * count,
        ),
        out_shape=[jax.ShapeDtypeStruct((cap, rows, SB), f32)] * count,
        compiler_params=params(),
        cost_estimate=cost(0, 4 * vector.size + 4 * count * cap * rows * SB),
        name="gather_blocks",
    )(lists, vector)


def beta_sum(vector, received, slots, own_signs, far_signs, pair_index, pair_tables, with_dot):
    rows, cols = vector.shape
    blocks = cols // SB
    npair = pair_tables.shape[0]
    kb = slots.shape[0]
    cap = received[0].shape[0]
    far = len(received)
    per = divisor(blocks, 16)
    steps = blocks // per

    def kernel(slots_ref, own_ref, far_ref, pair_ref, *refs):
        v_ref, t_ref = refs[:2]
        r_refs = refs[2 : 2 + far]
        outs = refs[2 + far : -5]
        pool, wide, t_high, t_low, sems = refs[-5:]
        g = pl.program_id(0)

        @pl.when(g == 0)
        def _():
            copies = [
                pltpu.make_async_copy(r_refs[i], pool.at[pl.ds(i * cap, cap)], sems.at[i]) for i in range(far)
            ]
            for copy in copies:
                copy.start()
            for p in range(npair):
                high, low = halves(t_ref[p])
                t_high[p * SB : (p + 1) * SB, :] = high
                t_low[p * SB : (p + 1) * SB, :] = low
            for copy in copies:
                copy.wait()

        wide[...] = jnp.zeros_like(wide)
        for t in range(per):
            target = g * per + t
            for k in range(kb):
                slot = slots_ref[k, target]
                own = v_ref[:, pl.ds(pl.multiple_of(lax.min(slot, blocks - 1) * SB, SB), SB)]
                other = pool[lax.max(slot - blocks, 0)]
                block = own * own_ref[k, target].astype(f32) + other * far_ref[k, target].astype(f32)
                at = pl.ds(pl.multiple_of(pair_ref[k, target] * SB, SB), SB)
                wide[t * rows : (t + 1) * rows, at] += block
        high, low = halves(wide[...])
        total = mul(high, t_high[...]) + mul(low, t_high[...]) + mul(high, t_low[...])
        dot = jnp.zeros((rows, SB), f32)
        square = jnp.zeros((rows, SB), f32)
        for t in range(per):
            piece = total[t * rows : (t + 1) * rows]
            outs[0][:, t * SB : (t + 1) * SB] = piece
            if with_dot:
                v = v_ref[:, pl.ds(pl.multiple_of((g * per + t) * SB, SB), SB)]
                dot = dot + piece * v
                square = square + v * v
        if with_dot:

            @pl.when(g == 0)
            def _():
                outs[1][...] = dot
                outs[2][...] = square

            @pl.when(g > 0)
            def _():
                outs[1][...] += dot
                outs[2][...] += square

    out = pl.pallas_call(
        kernel,
        grid_spec=pltpu.PrefetchScalarGridSpec(
            num_scalar_prefetch=4,
            grid=(steps,),
            in_specs=[
                pl.BlockSpec((rows, cols), lambda g, *_: (0, 0)),
                pl.BlockSpec(pair_tables.shape, lambda g, *_: (0, 0, 0)),
            ]
            + [pl.BlockSpec(memory_space=pl.ANY)] * far,
            out_specs=[pl.BlockSpec((rows, per * SB), lambda g, *_: (0, g))]
            + ([pl.BlockSpec((rows, SB), lambda g, *_: (0, 0))] * 2 if with_dot else []),
            scratch_shapes=[
                pltpu.VMEM((far * cap, rows, SB), f32),
                pltpu.VMEM((per * rows, npair * SB), f32),
                pltpu.VMEM((npair * SB, SB), bf16),
                pltpu.VMEM((npair * SB, SB), bf16),
                pltpu.SemaphoreType.DMA((far,)),
            ],
        ),
        out_shape=[jax.ShapeDtypeStruct((rows, cols), f32)]
        + ([jax.ShapeDtypeStruct((rows, SB), f32)] * 2 if with_dot else []),
        compiler_params=params(),
        cost_estimate=cost(6 * rows * cols * npair * SB, 4 * (2 * rows * cols + far * cap * rows * SB)),
        name="beta_sum",
    )(slots, own_signs, far_signs, pair_index, vector, pair_tables, *received)
    if with_dot:
        return out[0], jnp.stack([jnp.sum(out[1]), jnp.sum(out[2])])
    return out[0], None


def finish(returned, beta_term, place, chunk, n, width, previous, extra=None):
    rows, cols = beta_term.shape
    blocks = width // SB
    steps = divisor(blocks, 2)
    wide = width // steps
    full = 1 if extra is None else 3

    def kernel(place_ref, *refs):
        refs = list(refs)
        theta_ref = None
        if extra is not None:
            theta_ref = refs.pop(0)
        fulls = refs[:full]
        parts = refs[full : full + n]
        outs = refs[full + n + (previous is not None) :]
        k = pl.program_id(0)
        for i in range(n):

            @pl.when(k == i)
            def _(i=i):
                value = fulls[0][...] + parts[i][...]
                if extra is not None:
                    value = (value - theta_ref[0] * fulls[1][...]) / fulls[2][...]
                    outs[1 + (n - i) % n][...] = value
                outs[0][...] = value

    def whole(k, g, place):
        return (0, (chunk * n + lax.rem(place[0] + n - k, n)) * steps + g)

    def only(i):
        return lambda k, g, place: (0, jnp.where(k == i, g, jnp.where(k < i, 0, steps - 1)))

    in_specs = [pl.BlockSpec((rows, wide), whole)] * full + [pl.BlockSpec((rows, wide), only(i)) for i in range(n)]
    arrays = [beta_term] + ([] if extra is None else [extra[1], extra[2]]) + list(returned)
    if extra is not None:
        in_specs = [pl.BlockSpec(memory_space=pltpu.SMEM)] + in_specs
        arrays = [extra[0]] + arrays
    aliases = {}
    if previous is not None:
        aliases = {1 + len(arrays): 0}
        in_specs = in_specs + [pl.BlockSpec(memory_space=pl.ANY)]
        arrays = arrays + [previous]
    out_specs = [pl.BlockSpec((rows, wide), whole)]
    out_shape = [jax.ShapeDtypeStruct((rows, cols), f32)]
    if extra is not None:
        out_specs += [pl.BlockSpec((rows, wide), only((n - m) % n)) for m in range(n)]
        out_shape += [jax.ShapeDtypeStruct((rows, width), f32)] * n
    out = pl.pallas_call(
        kernel,
        grid_spec=pltpu.PrefetchScalarGridSpec(
            num_scalar_prefetch=1,
            grid=(n, steps),
            in_specs=in_specs,
            out_specs=out_specs,
        ),
        out_shape=out_shape,
        input_output_aliases=aliases,
        compiler_params=params(),
        cost_estimate=cost(4 * rows * n * width, 4 * (2 * full + 2) * rows * n * width),
        name="finish" if extra is None else "correct",
    )(place, *arrays)
    return out if extra is not None else out[0]


def plan(source_blocks, phase_signs, blocks, parts, cap):
    me = lax.axis_index("beta")
    everyone = lax.all_gather(source_blocks, "beta", axis=0, tiled=True).reshape(parts, -1)
    ids = jnp.arange(parts * blocks, dtype=jnp.int32)
    need = jnp.any(everyone[:, :, None] == ids, axis=1)
    need = need.reshape(parts, parts, blocks)
    order = jnp.arange(blocks, dtype=jnp.int32)
    before = (order[:, None] < order[None, :]).astype(bf16)
    position = jnp.dot(
        need.astype(bf16).reshape(parts * parts, blocks), before, preferred_element_type=f32
    ).astype(jnp.int32).reshape(parts, parts, blocks)
    counts = jnp.sum(need.astype(jnp.int32), axis=2)
    apart = 1 - jnp.eye(parts, dtype=jnp.int32)
    rounds_needed = (jnp.max(counts * apart) + cap - 1) // cap
    partners = me ^ jnp.arange(1, parts, dtype=jnp.int32)
    send_need = need[partners, me]
    send_position = position[partners, me]
    take_position = position[me].reshape(-1)
    sources = source_blocks.T
    own = sources // blocks == me
    far_index = (sources // blocks) ^ me
    found = jnp.sum(jnp.where(sources[:, :, None] == ids, take_position, 0), axis=2)
    signs = phase_signs.T

    def round_plan(r):
        slot = jnp.arange(cap, dtype=jnp.int32)[:, None] + r * cap
        hit = send_need[:, None, :] & (send_position[:, None, :] == slot)
        lists = jnp.sum(jnp.where(hit, order, 0), axis=2)
        here = (found >= r * cap) & (found < (r + 1) * cap)
        slots = jnp.where(own, sources - me * blocks, blocks + (far_index - 1) * cap + jnp.where(here, found - r * cap, 0))
        own_signs = jnp.where(own & (r == 0), signs, 0)
        far_signs = jnp.where(~own & here, signs, 0)
        return lists, slots, own_signs, far_signs

    return rounds_needed, round_plan


def make_local(n_alpha, n_beta):
    n = n_alpha // 2

    def local(
        start_vector,
        precondition,
        alpha_hamiltonian,
        alpha_pairs,
        pair_tables,
        source_blocks,
        pair_index,
        phase_signs,
        cross_pairs,
        cross_signs,
    ):
        rows, cols = start_vector.shape
        blocks = cols // SB
        chunks = divisor(blocks // n, CHUNKS)
        width = cols // (n * chunks)
        cap = (blocks + 1) // 2
        device = lax.axis_index("alpha")
        core = lax.rem(device, 2)
        place = (device // 2).astype(jnp.int32).reshape(1)
        nq = alpha_pairs.shape[0]

        stacked = jnp.concatenate([alpha_hamiltonian[None], alpha_pairs]).reshape(nq + 1, n, 2, rows, n, 2, rows)
        flipped = stacked[:, :, ::-1, :, :, ::-1]
        chosen = jnp.where(core == 0, stacked, flipped)[:, :, :, :, :, 0]
        couplings = jnp.transpose(chosen, (2, 1, 3, 0, 4, 5)).reshape(2 * n * rows, (nq + 1) * n * rows)
        pairs_by_k = pair_index.T

        def exchange(parts):
            return [
                lax.ppermute(part, "beta", [(i, i ^ k) for i in range(n_beta)]) for k, part in enumerate(parts, 1)
            ]

        rounds_needed, round_plan = plan(source_blocks, phase_signs, blocks, n_beta, cap)
        first_plan = round_plan(0)

        def beta_round(vector, planned, with_dot):
            lists, slots, own_signs, far_signs = planned
            received = exchange(gather_blocks(vector, lists))
            return beta_sum(vector, received, slots, own_signs, far_signs, pairs_by_k, pair_tables, with_dot)

        def beta_side(vector, with_dot):
            done = beta_round(vector, first_plan, with_dot)

            def more(done):
                added = beta_round(vector, round_plan(1), with_dot)
                total = done[0] + added[0]
                if with_dot:
                    return total, jnp.stack([done[1][0] + added[1][0], done[1][1]])
                return total, None

            return lax.cond(rounds_needed > 1, more, lambda done: done, done)

        def alpha_side(own, own_chunk, sent, chunk, with_dot):
            received = rotate(sent, n)
            mine, other = alpha_partial(
                own, own_chunk, received, couplings, pair_tables, cross_pairs, cross_signs, place, chunk, n, width
            )
            other = lax.ppermute(other, "alpha", [(i, i ^ 1) for i in range(n_alpha)])
            vectors = [(own, own_chunk)] + received if with_dot else []
            joined, dot = join(mine, other, vectors, place, n, width, with_dot)
            return [joined[0]] + rotate(joined[1:], n), dot

        returned = []
        dots = []
        for c in range(chunks):
            sent = pack(start_vector, place, c, n, width)
            back, dot = alpha_side(start_vector, c, sent, c, True)
            returned.append(back)
            dots.append(dot)
        beta_term, sums = beta_side(start_vector, True)
        mine = jnp.stack([jnp.full((8, SB), sum(dots) + sums[0]), jnp.full((8, SB), sums[1])])
        both = jnp.sum(lax.all_gather(mine, ("alpha", "beta"))[:, :, 0, 0], axis=0)
        theta = (both[0] / both[1]).reshape(1)

        correction = None
        sent = []
        for c in range(chunks):
            out = finish(
                returned[c], beta_term, place, c, n, width, correction, (theta, start_vector, precondition)
            )
            correction = out[0]
            sent.append(out[1:])
        returned = [alpha_side(sent[c][0], None, sent[c][1:], c, False)[0] for c in range(chunks)]
        beta_term, _ = beta_side(correction, False)
        sigma_next = None
        for c in range(chunks):
            sigma_next = finish(returned[c], beta_term, place, c, n, width, sigma_next)
        return correction, sigma_next

    return local


def solution(mesh):
    placed = (
        P("alpha", "beta"),
        P("alpha", "beta"),
        P(),
        P(),
        P(),
        P("beta", None),
        P("beta", None),
        P("beta", None),
        P(None, "beta"),
        P(None, "beta"),
    )
    return jax.shard_map(
        make_local(mesh.shape["alpha"], mesh.shape["beta"]),
        mesh=mesh,
        in_specs=placed,
        out_specs=(P("alpha", "beta"), P("alpha", "beta")),
        check_vma=False,
    )
```

```python
import jax
import jax.numpy as jnp
from jax import lax
from jax.experimental import pallas as pl
from jax.experimental.pallas import tpu as pltpu
from jax.sharding import PartitionSpec as P

SB = 128
CHUNKS = 1
VMEM_BYTES = 60 * 1024 * 1024
f32 = jnp.float32
bf16 = jnp.bfloat16


def params():
    return pltpu.CompilerParams(vmem_limit_bytes=VMEM_BYTES)


def divisor(number, most):
    return max(d for d in range(1, most + 1) if number % d == 0)


def halves(x):
    high = x.astype(bf16)
    return high, (x - high.astype(f32)).astype(bf16)


def mul(a, b):
    return jnp.dot(a, b, preferred_element_type=f32)


def cost(flops, count):
    return pl.CostEstimate(flops=1, bytes_accessed=1, transcendentals=0)


def prepare(alpha_hamiltonian, alpha_pairs, pair_tables, after):
    size = alpha_hamiltonian.shape[0]
    nq = alpha_pairs.shape[0]
    depth = (nq + 1) * size
    npair = pair_tables.shape[0]

    def kernel(h_ref, p_ref, t_ref, *refs):
        a_twice, a_low, t_high, t_low = refs[-4:]
        for q in range(nq + 1):
            high, low = halves(h_ref[...] if q == 0 else p_ref[q - 1])
            a_twice[:, q * size : (q + 1) * size] = high
            a_twice[:, depth + q * size : depth + (q + 1) * size] = high
            a_low[:, q * size : (q + 1) * size] = low
        for p in range(npair):
            high, low = halves(t_ref[p])
            t_high[p, :SB, :] = high
            t_high[p, SB:, :] = high
            t_low[p] = low

    shapes = [(size, 2 * depth), (size, depth), (npair, 2 * SB, SB), (npair, SB, SB)]
    return pl.pallas_call(
        kernel,
        in_specs=[pl.BlockSpec(memory_space=pltpu.VMEM)] * 3 + [pl.BlockSpec(memory_space=pl.ANY)] * len(after),
        out_specs=[pl.BlockSpec(memory_space=pltpu.VMEM)] * 4,
        out_shape=[jax.ShapeDtypeStruct(shape, bf16) for shape in shapes],
        compiler_params=params(),
        cost_estimate=cost(0, 0),
        name="prepare",
    )(alpha_hamiltonian, alpha_pairs, pair_tables, *after)


def pack(vector, chunk, parts, width):
    rows = vector.shape[0]

    def kernel(source, target):
        target[0] = source[...]

    return pl.pallas_call(
        kernel,
        grid=(parts,),
        in_specs=[pl.BlockSpec((rows, width), lambda j: (0, chunk * parts + j))],
        out_specs=pl.BlockSpec((1, rows, width), lambda j: (j, 0, 0)),
        out_shape=jax.ShapeDtypeStruct((parts, rows, width), f32),
        compiler_params=params(),
        cost_estimate=cost(0, 0),
        name="pack",
    )(vector)


def alpha_sum(columns, prepared, cross_pairs, cross_signs, device, chunk, parts, with_dot, after):
    size, width = columns.shape
    depth = prepared[1].shape[1]
    nq = cross_pairs.shape[0]
    blocks = width // SB
    per = divisor(blocks, 4)
    steps = blocks // per
    wide = per * SB

    def kernel(device_ref, pairs_ref, signs_ref, v_ref, a_twice, a_low, t_high, t_low, *refs):
        b = refs[-1]
        out_ref = refs[len(after)]
        g = pl.program_id(0)
        high, low = halves(v_ref[...])
        b[:size, :] = high
        b[depth : depth + size, :] = low
        first = (chunk * parts + device_ref[0]) * blocks + g * per
        for t in range(per):
            at = slice(t * SB, (t + 1) * SB)
            high = b[:size, at]
            both = jnp.concatenate([high, b[depth : depth + size, at]], axis=1)
            chosen = [pairs_ref[q, first + t] for q in range(nq)]
            x = mul(both, jnp.concatenate([t_high[p] for p in chosen], axis=1))
            x = x + mul(high, jnp.concatenate([t_low[p] for p in chosen], axis=1))
            for q in range(nq):
                x_high, x_low = halves(x[:, q * SB : (q + 1) * SB] * signs_ref[q, first + t].astype(f32))
                row = (q + 1) * size
                b[row : row + size, at] = x_high
                b[depth + row : depth + row + size, at] = x_low
        total = mul(a_twice[...], b[...]) + mul(a_low[...], b[:depth, :])
        out_ref[...] = total
        if with_dot:
            refs[-2][...] = jnp.sum(total * v_ref[...], axis=0, keepdims=True)

    column_spec = pl.BlockSpec((size, wide), lambda g, *_: (0, g))
    out = pl.pallas_call(
        kernel,
        grid_spec=pltpu.PrefetchScalarGridSpec(
            num_scalar_prefetch=3,
            grid=(steps,),
            in_specs=[column_spec]
            + [pl.BlockSpec(a.shape, lambda g, *_, zeros=(0,) * a.ndim: zeros) for a in prepared]
            + [pl.BlockSpec(memory_space=pl.ANY)] * len(after),
            out_specs=[column_spec] + ([pl.BlockSpec((1, wide), lambda g, *_: (0, g))] if with_dot else []),
            scratch_shapes=[pltpu.VMEM((2 * depth, wide), bf16)],
        ),
        out_shape=[jax.ShapeDtypeStruct((size, width), f32)]
        + ([jax.ShapeDtypeStruct((1, width), f32)] if with_dot else []),
        compiler_params=params(),
        cost_estimate=cost(0, 0),
        name="alpha_sum",
    )(device, cross_pairs, cross_signs, columns, *prepared, *after)
    return out[0], (out[1] if with_dot else None)


def earlier(lanes):
    row = lax.broadcasted_iota(jnp.int32, (lanes, lanes), 0)
    column = lax.broadcasted_iota(jnp.int32, (lanes, lanes), 1)
    return jnp.where(row < column, 1.0, 0.0).astype(bf16)


def mark(source_blocks, me, parts, after):
    blocks, kb = source_blocks.shape
    lanes = -(-blocks // SB) * SB
    tall = -(-parts // 8) * 8

    def kernel(me_ref, source_ref, *refs):
        marks_refs = refs[len(after) : len(after) + parts - 1]
        found_ref, held = refs[-2:]
        lane = lax.broadcasted_iota(jnp.int32, (blocks, lanes), 1)

        def hit(s, k):
            return (source_ref[:, k : k + 1] - s * blocks == lane) & (lane < blocks)

        held[...] = jnp.zeros_like(held)
        worst = jnp.zeros((1, 1), f32)
        for s in range(parts):
            needed = jnp.zeros((1, lanes), f32)
            for k in range(kb):
                needed = jnp.maximum(needed, jnp.max(jnp.where(hit(s, k), 1.0, 0.0), axis=0, keepdims=True))
            held[s : s + 1, :] = needed
            count = jnp.sum(needed, axis=1, keepdims=True)
            worst = jnp.maximum(worst, jnp.where(me_ref[0] == s, 0.0, count))
        place = mul(held[...].astype(bf16), earlier(lanes))
        for k in range(kb):
            found = jnp.zeros((blocks, 1), f32)
            for s in range(parts):
                found = found + jnp.sum(jnp.where(hit(s, k), place[s : s + 1, :], 0.0), axis=1, keepdims=True)
            found_ref[:, k : k + 1] = found.astype(jnp.int32)
        for k, marks_ref in enumerate(marks_refs, 1):
            marks_ref[...] = jnp.zeros_like(marks_ref)
            marks_ref[0:1, :] = held[pl.ds(me_ref[0] ^ k, 1), :]
            marks_ref[1:2, :] = jnp.broadcast_to(worst, (1, lanes))

    return pl.pallas_call(
        kernel,
        in_specs=[pl.BlockSpec(memory_space=pltpu.SMEM), pl.BlockSpec(memory_space=pltpu.VMEM)]
        + [pl.BlockSpec(memory_space=pl.ANY)] * len(after),
        out_specs=[pl.BlockSpec(memory_space=pltpu.VMEM)] * parts,
        out_shape=[jax.ShapeDtypeStruct((8, lanes), f32)] * (parts - 1)
        + [jax.ShapeDtypeStruct((blocks, kb), jnp.int32)],
        scratch_shapes=[pltpu.VMEM((tall, lanes), f32)],
        compiler_params=params(),
        cost_estimate=cost(0, 0),
        name="mark",
    )(me, source_blocks, *after)


def positions(marks, first, cap):
    lanes = marks[0].shape[1]
    count = len(marks)
    tall = -(-count // 8) * 8

    def kernel(*refs):
        out_ref, held = refs[-2:]
        held[...] = jnp.zeros_like(held)
        for k in range(count):
            held[k : k + 1, :] = refs[k][0:1, :]
        needed = held[...]
        slot = mul(needed.astype(bf16), earlier(lanes)).astype(jnp.int32) - first
        out_ref[...] = jnp.where((needed > 0) & (slot >= 0) & (slot < cap), slot, cap)

    return pl.pallas_call(
        kernel,
        in_specs=[pl.BlockSpec(memory_space=pltpu.VMEM)] * count,
        out_specs=pl.BlockSpec(memory_space=pltpu.VMEM),
        out_shape=jax.ShapeDtypeStruct((tall, lanes), jnp.int32),
        scratch_shapes=[pltpu.VMEM((tall, lanes), f32)],
        compiler_params=params(),
        cost_estimate=cost(0, 0),
        name="positions",
    )(*marks)


def gather_blocks(vector, slots, count, cap, after):
    rows, cols = vector.shape

    def kernel(slots_ref, v_ref, *refs):
        outs = refs[len(after) :]

        @pl.loop(0, cols // SB, unroll=4)
        def _(b):
            block = v_ref[:, pl.ds(pl.multiple_of(b * SB, SB), SB)]
            for k in range(count):
                outs[k][slots_ref[k, b]] = block

    shape = (cap + 1, rows, SB)
    return pl.pallas_call(
        kernel,
        grid_spec=pltpu.PrefetchScalarGridSpec(
            num_scalar_prefetch=1,
            grid=(1,),
            in_specs=[pl.BlockSpec(vector.shape, lambda g, *_: (0, 0))]
            + [pl.BlockSpec(memory_space=pl.ANY)] * len(after),
            out_specs=[pl.BlockSpec(shape, lambda g, *_: (0, 0, 0))] * count,
        ),
        out_shape=[jax.ShapeDtypeStruct(shape, f32)] * count,
        compiler_params=params(),
        cost_estimate=cost(0, 0),
        name="gather_blocks",
    )(slots, vector, *after)


def beta_sum(vector, received, slots, signs, pair_index, pair_tables, after, dots=None, with_dot=False):
    rows, cols = vector.shape
    blocks = cols // SB
    npair = pair_tables.shape[0]
    kb = slots.shape[0]
    far = len(received)
    each = received[0].shape[0]
    dots = [] if dots is None else dots
    per = divisor(blocks, 16)
    steps = blocks // per

    def kernel(slots_ref, sign_ref, pair_ref, *refs):
        v_ref, t_ref = refs[:2]
        r_refs = refs[2 : 2 + far]
        at = 2 + far + len(after)
        dot_refs = refs[at : at + len(dots)]
        out_ref = refs[at + len(dots)]
        pool, wide, t_high, t_low, sems = refs[-5:]
        g = pl.program_id(0)

        @pl.when(g == 0)
        def _():
            copies = [
                pltpu.make_async_copy(r_refs[i], pool.at[pl.ds(i * each, each)], sems.at[i]) for i in range(far)
            ]
            for copy in copies:
                copy.start()
            for p in range(npair):
                high, low = halves(t_ref[p])
                t_high[p * SB : (p + 1) * SB, :] = high
                t_low[p * SB : (p + 1) * SB, :] = low
            for copy in copies:
                copy.wait()

        wide[...] = jnp.zeros_like(wide)
        for t in range(per):
            target = g * per + t
            for k in range(kb):
                slot = slots_ref[k, target]
                own = v_ref[:, pl.ds(pl.multiple_of(lax.min(slot, blocks - 1) * SB, SB), SB)]
                other = pool[lax.max(slot - blocks, 0)]
                block = jnp.where(slot < blocks, own, other) * sign_ref[k, target].astype(f32)
                at = pl.ds(pl.multiple_of(pair_ref[k, target] * SB, SB), SB)
                wide[t * rows : (t + 1) * rows, at] += block
        high, low = halves(wide[...])
        total = mul(high, t_high[...]) + mul(low, t_high[...]) + mul(high, t_low[...])
        for t in range(per):
            out_ref[:, t * SB : (t + 1) * SB] = total[t * rows : (t + 1) * rows]
        if with_dot:
            sums_ref = refs[-6]
            dot = jnp.zeros((rows, SB), f32)
            square = jnp.zeros((rows, SB), f32)
            for t in range(per):
                v = v_ref[:, pl.ds(pl.multiple_of((g * per + t) * SB, SB), SB)]
                dot = dot + total[t * rows : (t + 1) * rows] * v
                square = square + v * v
            dot = jnp.sum(dot, axis=0, keepdims=True)
            square = jnp.sum(square, axis=0, keepdims=True)

            @pl.when(g == 0)
            def _():
                sums_ref[...] = jnp.zeros_like(sums_ref)

            sums_ref[0:1, :] += dot
            if dots:
                sums_ref[1:2, :] += square

            @pl.when(g == steps - 1)
            def _():
                value = sums_ref[...]
                for ref in dot_refs:
                    for at in range(0, ref.shape[1], SB):
                        first = lax.broadcasted_iota(jnp.int32, value.shape, 0) == 0
                        value = value + jnp.where(first, ref[:, at : at + SB], 0.0)
                sums_ref[...] = value

    out = pl.pallas_call(
        kernel,
        grid_spec=pltpu.PrefetchScalarGridSpec(
            num_scalar_prefetch=3,
            grid=(steps,),
            in_specs=[
                pl.BlockSpec((rows, cols), lambda g, *_: (0, 0)),
                pl.BlockSpec(pair_tables.shape, lambda g, *_: (0, 0, 0)),
            ]
            + [pl.BlockSpec(memory_space=pl.ANY)] * (far + len(after))
            + [pl.BlockSpec(dot.shape, lambda g, *_: (0, 0)) for dot in dots],
            out_specs=[pl.BlockSpec((rows, per * SB), lambda g, *_: (0, g))]
            + ([pl.BlockSpec((8, SB), lambda g, *_: (0, 0))] if with_dot else []),
            scratch_shapes=[
                pltpu.VMEM((far * each, rows, SB), f32),
                pltpu.VMEM((per * rows, npair * SB), f32),
                pltpu.VMEM((npair * SB, SB), bf16),
                pltpu.VMEM((npair * SB, SB), bf16),
                pltpu.SemaphoreType.DMA((far,)),
            ],
        ),
        out_shape=[jax.ShapeDtypeStruct((rows, cols), f32)]
        + ([jax.ShapeDtypeStruct((8, SB), f32)] if with_dot else []),
        compiler_params=params(),
        cost_estimate=cost(0, 0),
        name="beta_sum",
    )(slots, signs, pair_index, vector, pair_tables, *received, *after, *dots)
    return list(out)


def finish(returned, beta_term, chunk, parts, width, previous, extra=None):
    rows, cols = beta_term.shape
    full = 1 if extra is None else 3
    sums = [] if extra is None else extra[0]

    def kernel(*refs):
        refs = list(refs)
        if extra is not None:
            sum_refs = refs[: len(sums)]
            del refs[: len(sums)]
            theta_ref = refs.pop()

            @pl.when(pl.program_id(0) == 0)
            def _():
                total = sum_refs[0][...]
                for ref in sum_refs[1:]:
                    total = total + ref[...]
                both = [jnp.sum(total[i : i + 1], axis=1, keepdims=True) for i in range(2)]
                theta_ref[...] = jnp.broadcast_to(both[0] / both[1], theta_ref.shape)

        value = refs[0][...] + refs[full][0]
        outs = refs[full + 1 + (previous is not None) :]
        if extra is not None:
            value = (value - theta_ref[0:1, 0:1] * refs[1][...]) / refs[2][...]
            outs[1][0] = value
        outs[0][...] = value

    whole = pl.BlockSpec((rows, width), lambda j: (0, chunk * parts + j))
    part = pl.BlockSpec((1, rows, width), lambda j: (j, 0, 0))
    in_specs = [pl.BlockSpec(a.shape, lambda j: (0, 0)) for a in sums] + [whole] * full + [part]
    arrays = list(sums) + [beta_term] + ([] if extra is None else [extra[1], extra[2]]) + [returned]
    aliases = {}
    if previous is not None:
        aliases = {len(arrays): 0}
        in_specs = in_specs + [pl.BlockSpec(memory_space=pl.ANY)]
        arrays = arrays + [previous]
    out_specs = [whole]
    out_shape = [jax.ShapeDtypeStruct((rows, cols), f32)]
    if extra is not None:
        out_specs += [part]
        out_shape += [jax.ShapeDtypeStruct((parts, rows, width), f32)]
    return pl.pallas_call(
        kernel,
        grid=(parts,),
        in_specs=in_specs,
        out_specs=out_specs,
        scratch_shapes=[] if extra is None else [pltpu.VMEM((8, SB), f32)],
        out_shape=out_shape,
        input_output_aliases=aliases,
        compiler_params=params(),
        cost_estimate=cost(0, 0),
        name="finish" if extra is None else "correct",
    )(*arrays)


def make_local(n_alpha, n_beta):
    chips = n_alpha // 2

    def to_partners(parts):
        return [lax.ppermute(part, "beta", [(i, i ^ k) for i in range(n_beta)]) for k, part in enumerate(parts, 1)]

    def turn(parts):
        return lax.all_to_all(parts, "alpha", 0, 0, tiled=True)

    def local(
        start_vector,
        precondition,
        alpha_hamiltonian,
        alpha_pairs,
        pair_tables,
        source_blocks,
        pair_index,
        phase_signs,
        cross_pairs,
        cross_signs,
    ):
        rows, cols = start_vector.shape
        blocks = cols // SB
        chunks = divisor(blocks // n_alpha, CHUNKS)
        width = cols // (n_alpha * chunks)
        cap = (blocks + 1) // 2
        device = lax.axis_index("alpha").astype(jnp.int32).reshape(1)
        me = lax.axis_index("beta").astype(jnp.int32)

        sent = [pack(start_vector, c, n_alpha, width) for c in range(chunks)]
        arrived = [turn(parts) for parts in sent]

        *marks, found = mark(source_blocks, me.reshape(1), n_beta, sent[:1])
        worst = marks[0][1:2, :1]
        marks = to_partners(marks)
        for other in marks:
            worst = jnp.maximum(worst, other[1:2, :1])
        too_many = worst[0, 0] > cap
        pairs_by_k = pair_index.T

        def plan(r):
            partner = (source_blocks // blocks) ^ me
            here = (found >= r * cap) & (found < (r + 1) * cap) & (partner != 0)
            far_slot = blocks + (partner - 1) * (cap + 1) + found - r * cap
            mine = (partner == 0) & (r == 0)
            slots = jnp.where(mine, source_blocks - me * blocks, jnp.where(here, far_slot, 0))
            signs = jnp.where(mine | here, phase_signs, 0)
            return positions(marks, r * cap, cap), slots.T, signs.T

        first_plan = plan(0)

        def beta_send(vector, planned, after):
            sent = gather_blocks(vector, planned[0], n_beta - 1, cap, after)
            received = to_partners(sent)
            return received, received[:2]

        def beta_round(vector, received, planned, after, dots=None, with_dot=False):
            _, slots, signs = planned
            return beta_sum(vector, received, slots, signs, pairs_by_k, pair_tables, after, dots, with_dot)

        def beta_side(vector, received, after, dots=None, with_dot=False):
            done = beta_round(vector, received, first_plan, after, dots, with_dot)

            def more(done):
                for r in range(1, -(-blocks // cap)):
                    planned = plan(r)
                    added = beta_round(vector, beta_send(vector, planned, [])[0], planned, [], None, with_dot)
                    done = [a + b for a, b in zip(done, added)]
                return done

            return lax.cond(too_many, more, lambda done: done, done)

        def alpha_side(arrived, with_dot, after):
            sides = []
            for c, parts in enumerate(arrived):
                columns = parts.reshape(n_alpha * rows, width)
                total, dot = alpha_sum(
                    columns, prepared, cross_pairs, cross_signs, device, c, n_alpha, with_dot, after
                )
                sides.append((turn(total.reshape(n_alpha, rows, width)), dot, total))
            return sides

        received, token = beta_send(start_vector, first_plan, [])
        prepared = prepare(alpha_hamiltonian, alpha_pairs, pair_tables, [])
        sides = alpha_side(arrived, True, token)
        beta_term, sums = beta_side(start_vector, received, [], [side[1] for side in sides], True)
        for other in to_partners([sums] * (n_beta - 1)):
            sums = sums + other
        sums = sums + lax.ppermute(sums, "alpha", [(i, i ^ 1) for i in range(n_alpha)])
        all_sums = [sums]
        for k in range(1, chips):
            pairs = [(i, ((i // 2 + k) % chips) * 2 + i % 2) for i in range(n_alpha)]
            all_sums.append(lax.ppermute(sums, "alpha", pairs))

        correction = None
        arrived = []
        for c in range(chunks):
            extra = (all_sums, start_vector, precondition)
            correction, parts = finish(sides[c][0], beta_term, c, n_alpha, width, correction, extra)
            arrived.append(turn(parts))
        received, token = beta_send(correction, first_plan, [])
        sides = alpha_side(arrived, False, token)
        (beta_term,) = beta_side(correction, received, [side[2] for side in sides])
        sigma_next = None
        for c in range(chunks):
            (sigma_next,) = finish(sides[c][0], beta_term, c, n_alpha, width, sigma_next)
        return correction, sigma_next

    return local


def solution(mesh):
    placed = (
        P("alpha", "beta"),
        P("alpha", "beta"),
        P(),
        P(),
        P(),
        P("beta", None),
        P("beta", None),
        P("beta", None),
        P(None, "beta"),
        P(None, "beta"),
    )
    return jax.shard_map(
        make_local(mesh.shape["alpha"], mesh.shape["beta"]),
        mesh=mesh,
        in_specs=placed,
        out_specs=(P("alpha", "beta"), P("alpha", "beta")),
        check_vma=False,
    )
```

```python
import jax
import jax.numpy as jnp
from jax import lax
from jax.experimental import pallas as pl
from jax.experimental.pallas import tpu as pltpu
from jax.sharding import PartitionSpec as P

SB = 128
VMEM_BYTES = 60 * 1024 * 1024
f32 = jnp.float32
bf16 = jnp.bfloat16


def params():
    return pltpu.CompilerParams(vmem_limit_bytes=VMEM_BYTES)


def divisor(number, most):
    return max(d for d in range(1, most + 1) if number % d == 0)


def halves(x):
    high = x.astype(bf16)
    return high, (x - high.astype(f32)).astype(bf16)


def mul(a, b):
    return jnp.dot(a, b, preferred_element_type=f32)


def cost(flops, count):
    return pl.CostEstimate(flops=1, bytes_accessed=1, transcendentals=0)


def prepare(alpha_hamiltonian, alpha_pairs, pair_tables, after):
    size = alpha_hamiltonian.shape[0]
    nq = alpha_pairs.shape[0]
    depth = (nq + 1) * size
    npair = pair_tables.shape[0]

    def kernel(h_ref, p_ref, t_ref, *refs):
        a_twice, a_low, t_high, t_low = refs[-4:]
        for q in range(nq + 1):
            high, low = halves(h_ref[...] if q == 0 else p_ref[q - 1])
            a_twice[:, q * size : (q + 1) * size] = high
            a_twice[:, depth + q * size : depth + (q + 1) * size] = high
            a_low[:, q * size : (q + 1) * size] = low
        for p in range(npair):
            high, low = halves(t_ref[p])
            t_high[p, :SB, :] = high
            t_high[p, SB:, :] = high
            t_low[p] = low

    shapes = [(size, 2 * depth), (size, depth), (npair, 2 * SB, SB), (npair, SB, SB)]
    return pl.pallas_call(
        kernel,
        in_specs=[pl.BlockSpec(memory_space=pltpu.VMEM)] * 3 + [pl.BlockSpec(memory_space=pl.ANY)] * len(after),
        out_specs=[pl.BlockSpec(memory_space=pltpu.VMEM)] * 4,
        out_shape=[jax.ShapeDtypeStruct(shape, bf16) for shape in shapes],
        compiler_params=params(),
        cost_estimate=cost(0, 0),
        name="prepare",
    )(alpha_hamiltonian, alpha_pairs, pair_tables, *after)


def pack(vector, parts):
    rows, cols = vector.shape
    width = cols // parts

    def kernel(source, target, held, sems):
        def taken(j):
            at = pl.ds(pl.multiple_of(j * width, SB), width)
            return pltpu.make_async_copy(source.at[:, at], held.at[j], sems.at[0, j])

        def given(j):
            return pltpu.make_async_copy(held.at[j], target.at[j], sems.at[1, j])

        for j in range(parts):
            taken(j).start()
        for j in range(parts):
            taken(j).wait()
            given(j).start()
        for j in range(parts):
            given(j).wait()

    return pl.pallas_call(
        kernel,
        in_specs=[pl.BlockSpec(memory_space=pl.ANY)],
        out_specs=pl.BlockSpec(memory_space=pl.ANY),
        out_shape=jax.ShapeDtypeStruct((parts, rows, width), f32),
        scratch_shapes=[pltpu.VMEM((parts, rows, width), f32), pltpu.SemaphoreType.DMA((2, parts))],
        compiler_params=params(),
        cost_estimate=cost(0, 0),
        name="pack",
    )(vector)


def alpha_sum(columns, prepared, cross_pairs, cross_signs, device, after):
    size, width = columns.shape
    depth = prepared[1].shape[1]
    nq = cross_pairs.shape[0]
    blocks = width // SB
    per = divisor(blocks, 8)
    steps = blocks // per
    wide = per * SB

    def kernel(device_ref, pairs_ref, signs_ref, v_any, *refs):
        prepared_any = refs[:4]
        out_any = refs[4 + len(after)]
        v_held, out_held, a_twice, a_low, t_high, t_low, even, odd, sems, once = refs[-10:]

        def at(g):
            return pl.ds(pl.multiple_of(g * wide, SB), wide)

        def taken(g):
            return pltpu.make_async_copy(v_any.at[:, at(g)], v_held.at[g], sems.at[0, g])

        def given(g):
            return pltpu.make_async_copy(out_held.at[g], out_any.at[:, at(g)], sems.at[1, g])

        held = (a_twice, a_low, t_high, t_low)
        loads = [pltpu.make_async_copy(prepared_any[i], held[i], once.at[i]) for i in range(4)]
        for load in loads[2:]:
            load.start()
        taken(0).start()
        for load in loads[:2]:
            load.start()
        for g in range(1, steps):
            taken(g).start()
        for load in loads[2:]:
            load.wait()

        def build(g, b):
            high, low = halves(v_held[g])
            b[:size, :] = high
            b[depth : depth + size, :] = low
            first = device_ref[0] * blocks + g * per
            for t in range(per):
                here = slice(t * SB, (t + 1) * SB)
                both = jnp.concatenate([high[:, here], low[:, here]], axis=1)
                chosen = [pairs_ref[q, first + t] for q in range(nq)]
                x = mul(both, jnp.concatenate([t_high[p] for p in chosen], axis=1))
                x = x + mul(high[:, here], jnp.concatenate([t_low[p] for p in chosen], axis=1))
                for q in range(nq):
                    x_high, x_low = halves(x[:, q * SB : (q + 1) * SB] * signs_ref[q, first + t].astype(f32))
                    row = (q + 1) * size
                    b[row : row + size, here] = x_high
                    b[depth + row : depth + row + size, here] = x_low

        taken(0).wait()
        build(0, even)
        for load in loads[:2]:
            load.wait()
        for g in range(steps):
            b, other = (even, odd) if g % 2 == 0 else (odd, even)
            if g + 1 < steps:
                taken(g + 1).wait()
                build(g + 1, other)
            out_held[g] = mul(a_twice[...], b[...]) + mul(a_low[...], b[:depth, :])
            given(g).start()
        for g in range(steps):
            given(g).wait()

    anywhere = pl.BlockSpec(memory_space=pl.ANY)
    return pl.pallas_call(
        kernel,
        in_specs=[pl.BlockSpec(memory_space=pltpu.SMEM)] * 3 + [anywhere] * (5 + len(after)),
        out_specs=anywhere,
        out_shape=jax.ShapeDtypeStruct((size, width), f32),
        scratch_shapes=[pltpu.VMEM((steps, size, wide), f32)] * 2
        + [pltpu.VMEM(a.shape, bf16) for a in prepared]
        + [
            pltpu.VMEM((2 * depth, wide), bf16),
            pltpu.VMEM((2 * depth, wide), bf16),
            pltpu.SemaphoreType.DMA((2, steps)),
            pltpu.SemaphoreType.DMA((4,)),
        ],
        compiler_params=params(),
        cost_estimate=cost(0, 0),
        name="alpha_sum",
    )(device, cross_pairs, cross_signs, columns, *prepared, *after)


def earlier(lanes):
    row = lax.broadcasted_iota(jnp.int32, (lanes, lanes), 0)
    column = lax.broadcasted_iota(jnp.int32, (lanes, lanes), 1)
    return jnp.where(row < column, 1.0, 0.0).astype(bf16)


def mark(source_blocks, me, parts, after):
    blocks, kb = source_blocks.shape
    lanes = -(-blocks // SB) * SB
    tall = -(-parts // 8) * 8

    def kernel(me_ref, source_ref, *refs):
        marks_refs = refs[len(after) : len(after) + parts - 1]
        found_ref, held = refs[-2:]
        lane = lax.broadcasted_iota(jnp.int32, (blocks, lanes), 1)

        def hit(s, k):
            return (source_ref[:, k : k + 1] - s * blocks == lane) & (lane < blocks)

        held[...] = jnp.zeros_like(held)
        worst = jnp.zeros((1, 1), f32)
        for s in range(parts):
            needed = jnp.zeros((1, lanes), f32)
            for k in range(kb):
                needed = jnp.maximum(needed, jnp.max(jnp.where(hit(s, k), 1.0, 0.0), axis=0, keepdims=True))
            held[s : s + 1, :] = needed
            count = jnp.sum(needed, axis=1, keepdims=True)
            worst = jnp.maximum(worst, jnp.where(me_ref[0] == s, 0.0, count))
        place = mul(held[...].astype(bf16), earlier(lanes))
        for k in range(kb):
            found = jnp.zeros((blocks, 1), f32)
            for s in range(parts):
                found = found + jnp.sum(jnp.where(hit(s, k), place[s : s + 1, :], 0.0), axis=1, keepdims=True)
            found_ref[:, k : k + 1] = found.astype(jnp.int32)
        for k, marks_ref in enumerate(marks_refs, 1):
            marks_ref[...] = jnp.zeros_like(marks_ref)
            marks_ref[0:1, :] = held[pl.ds(me_ref[0] ^ k, 1), :]
            marks_ref[1:2, :] = jnp.broadcast_to(worst, (1, lanes))

    return pl.pallas_call(
        kernel,
        in_specs=[pl.BlockSpec(memory_space=pltpu.SMEM), pl.BlockSpec(memory_space=pltpu.VMEM)]
        + [pl.BlockSpec(memory_space=pl.ANY)] * len(after),
        out_specs=[pl.BlockSpec(memory_space=pltpu.VMEM)] * parts,
        out_shape=[jax.ShapeDtypeStruct((8, lanes), f32)] * (parts - 1)
        + [jax.ShapeDtypeStruct((blocks, kb), jnp.int32)],
        scratch_shapes=[pltpu.VMEM((tall, lanes), f32)],
        compiler_params=params(),
        cost_estimate=cost(0, 0),
        name="mark",
    )(me, source_blocks, *after)


def positions(marks, first, cap):
    lanes = marks[0].shape[1]
    count = len(marks)
    tall = -(-count // 8) * 8

    def kernel(*refs):
        out_ref, held = refs[-2:]
        held[...] = jnp.zeros_like(held)
        for k in range(count):
            held[k : k + 1, :] = refs[k][0:1, :]
        needed = held[...]
        slot = mul(needed.astype(bf16), earlier(lanes)).astype(jnp.int32) - first
        out_ref[...] = jnp.where((needed > 0) & (slot >= 0) & (slot < cap), slot, cap)

    return pl.pallas_call(
        kernel,
        in_specs=[pl.BlockSpec(memory_space=pltpu.VMEM)] * count,
        out_specs=pl.BlockSpec(memory_space=pltpu.VMEM),
        out_shape=jax.ShapeDtypeStruct((tall, lanes), jnp.int32),
        scratch_shapes=[pltpu.VMEM((tall, lanes), f32)],
        compiler_params=params(),
        cost_estimate=cost(0, 0),
        name="positions",
    )(*marks)


def gather_blocks(vector, slots, count, cap, after):
    rows, cols = vector.shape

    def kernel(slots_ref, v_ref, *refs):
        outs = refs[len(after) :]

        @pl.loop(0, cols // SB, unroll=4)
        def _(b):
            block = v_ref[:, pl.ds(pl.multiple_of(b * SB, SB), SB)]
            for k in range(count):
                outs[k][slots_ref[k, b]] = block

    shape = (cap + 1, rows, SB)
    return pl.pallas_call(
        kernel,
        grid_spec=pltpu.PrefetchScalarGridSpec(
            num_scalar_prefetch=1,
            grid=(1,),
            in_specs=[pl.BlockSpec(vector.shape, lambda g, *_: (0, 0))]
            + [pl.BlockSpec(memory_space=pl.ANY)] * len(after),
            out_specs=[pl.BlockSpec(shape, lambda g, *_: (0, 0, 0))] * count,
        ),
        out_shape=[jax.ShapeDtypeStruct(shape, f32)] * count,
        compiler_params=params(),
        cost_estimate=cost(0, 0),
        name="gather_blocks",
    )(slots, vector, *after)


def beta_sum(vector, received, slots, signs, pair_index, pair_tables, after, dots=None, with_dot=False):
    rows, cols = vector.shape
    blocks = cols // SB
    npair = pair_tables.shape[0]
    kb = slots.shape[0]
    far = len(received)
    each = received[0].shape[0]
    dots = [] if dots is None else dots
    per = divisor(blocks, 16)
    steps = blocks // per

    def kernel(slots_ref, sign_ref, pair_ref, *refs):
        v_ref, t_ref = refs[:2]
        r_refs = refs[2 : 2 + far]
        at = 2 + far + len(after)
        dot_refs = refs[at : at + len(dots)]
        out_ref = refs[at + len(dots)]
        pool, wide, t_high, t_low, sems = refs[-5:]
        g = pl.program_id(0)

        @pl.when(g == 0)
        def _():
            copies = [
                pltpu.make_async_copy(r_refs[i], pool.at[pl.ds(i * each, each)], sems.at[i]) for i in range(far)
            ]
            for copy in copies:
                copy.start()
            for p in range(npair):
                high, low = halves(t_ref[p])
                t_high[p * SB : (p + 1) * SB, :] = high
                t_low[p * SB : (p + 1) * SB, :] = low
            for copy in copies:
                copy.wait()

        wide[...] = jnp.zeros_like(wide)
        for t in range(per):
            target = g * per + t
            for k in range(kb):
                slot = slots_ref[k, target]
                own = v_ref[:, pl.ds(pl.multiple_of(lax.min(slot, blocks - 1) * SB, SB), SB)]
                other = pool[lax.max(slot - blocks, 0)]
                block = jnp.where(slot < blocks, own, other) * sign_ref[k, target].astype(f32)
                at = pl.ds(pl.multiple_of(pair_ref[k, target] * SB, SB), SB)
                wide[t * rows : (t + 1) * rows, at] += block
        high, low = halves(wide[...])
        total = mul(high, t_high[...]) + mul(low, t_high[...]) + mul(high, t_low[...])
        for t in range(per):
            out_ref[:, t * SB : (t + 1) * SB] = total[t * rows : (t + 1) * rows]
        if with_dot:
            sums_ref = refs[-6]
            dot = jnp.zeros((rows, SB), f32)
            square = jnp.zeros((rows, SB), f32)
            for t in range(per):
                v = v_ref[:, pl.ds(pl.multiple_of((g * per + t) * SB, SB), SB)]
                dot = dot + total[t * rows : (t + 1) * rows] * v
                square = square + v * v
            dot = jnp.sum(dot, axis=0, keepdims=True)
            square = jnp.sum(square, axis=0, keepdims=True)

            @pl.when(g == 0)
            def _():
                sums_ref[...] = jnp.zeros_like(sums_ref)

            sums_ref[0:1, :] += dot
            if dots:
                sums_ref[1:2, :] += square

            @pl.when(g == steps - 1)
            def _():
                value = sums_ref[...]
                for ref in dot_refs:
                    for at in range(0, ref.shape[1], SB):
                        first = lax.broadcasted_iota(jnp.int32, value.shape, 0) == 0
                        value = value + jnp.where(first, ref[:, at : at + SB], 0.0)
                sums_ref[...] = value

    out = pl.pallas_call(
        kernel,
        grid_spec=pltpu.PrefetchScalarGridSpec(
            num_scalar_prefetch=3,
            grid=(steps,),
            in_specs=[
                pl.BlockSpec((rows, cols), lambda g, *_: (0, 0)),
                pl.BlockSpec(pair_tables.shape, lambda g, *_: (0, 0, 0)),
            ]
            + [pl.BlockSpec(memory_space=pl.ANY)] * (far + len(after))
            + [pl.BlockSpec(dot.shape, lambda g, *_: (0, 0)) for dot in dots],
            out_specs=[pl.BlockSpec((rows, per * SB), lambda g, *_: (0, g))]
            + ([pl.BlockSpec((8, SB), lambda g, *_: (0, 0))] if with_dot else []),
            scratch_shapes=[
                pltpu.VMEM((far * each, rows, SB), f32),
                pltpu.VMEM((per * rows, npair * SB), f32),
                pltpu.VMEM((npair * SB, SB), bf16),
                pltpu.VMEM((npair * SB, SB), bf16),
                pltpu.SemaphoreType.DMA((far,)),
            ],
        ),
        out_shape=[jax.ShapeDtypeStruct((rows, cols), f32)]
        + ([jax.ShapeDtypeStruct((8, SB), f32)] if with_dot else []),
        compiler_params=params(),
        cost_estimate=cost(0, 0),
        name="beta_sum",
    )(slots, signs, pair_index, vector, pair_tables, *received, *after, *dots)
    return list(out)


def finish(returned, beta_term, extra=None):
    rows, cols = beta_term.shape
    parts, _, width = returned.shape
    sums = [] if extra is None else extra[0]
    wholes = [beta_term] + ([] if extra is None else [extra[1], extra[2]])
    count = len(wholes)
    outs = 1 if extra is None else 2

    def kernel(*refs):
        sum_refs = refs[: len(sums)]
        whole_refs = refs[len(sums) : len(sums) + count]
        part_ref = refs[len(sums) + count]
        out_refs = refs[len(sums) + count + 1 :][:outs]
        held, sems, out_sems = refs[-3:]

        def at(j):
            return pl.ds(pl.multiple_of(j * width, SB), width)

        def taken(j):
            copies = [
                pltpu.make_async_copy(whole_refs[i].at[:, at(j)], held.at[i, j], sems.at[i, j]) for i in range(count)
            ]
            return copies + [pltpu.make_async_copy(part_ref.at[j], held.at[count, j], sems.at[count, j])]

        def given(j):
            copies = [pltpu.make_async_copy(held.at[count, j], out_refs[0].at[:, at(j)], out_sems.at[0, j])]
            if extra is not None:
                copies.append(pltpu.make_async_copy(held.at[count, j], out_refs[1].at[j], out_sems.at[1, j]))
            return copies

        for j in range(parts):
            for copy in taken(j):
                copy.start()
        theta = None
        if extra is not None:
            total = sum_refs[0][...]
            for ref in sum_refs[1:]:
                total = total + ref[...]
            both = [jnp.sum(total[i : i + 1], axis=1, keepdims=True) for i in range(2)]
            theta = both[0] / both[1]

        def step(j, _):
            for copy in taken(j):
                copy.wait()
            value = held[0, j] + held[count, j]
            if extra is not None:
                value = (value - theta * held[1, j]) / held[2, j]
            held[count, j] = value
            for copy in given(j):
                copy.start()
            return 0

        lax.fori_loop(0, parts, step, 0)
        for j in range(parts):
            for copy in given(j):
                copy.wait()

    anywhere = pl.BlockSpec(memory_space=pl.ANY)
    return pl.pallas_call(
        kernel,
        in_specs=[pl.BlockSpec(memory_space=pltpu.VMEM)] * len(sums) + [anywhere] * (count + 1),
        out_specs=[anywhere] * outs,
        out_shape=[jax.ShapeDtypeStruct((rows, cols), f32), jax.ShapeDtypeStruct((parts, rows, width), f32)][:outs],
        scratch_shapes=[
            pltpu.VMEM((count + 1, parts, rows, width), f32),
            pltpu.SemaphoreType.DMA((count + 1, parts)),
            pltpu.SemaphoreType.DMA((outs, parts)),
        ],
        compiler_params=params(),
        cost_estimate=cost(0, 0),
        name="finish" if extra is None else "correct",
    )(*sums, *wholes, returned)


def make_local(n_alpha, n_beta):
    chips = n_alpha // 2

    def to_partners(parts):
        return [lax.ppermute(part, "beta", [(i, i ^ k) for i in range(n_beta)]) for k, part in enumerate(parts, 1)]

    def turn(parts):
        return lax.all_to_all(parts, "alpha", 0, 0, tiled=True)

    def local(
        start_vector,
        precondition,
        alpha_hamiltonian,
        alpha_pairs,
        pair_tables,
        source_blocks,
        pair_index,
        phase_signs,
        cross_pairs,
        cross_signs,
    ):
        rows, cols = start_vector.shape
        blocks = cols // SB
        width = cols // n_alpha
        cap = (blocks + 1) // 2
        device = lax.axis_index("alpha").astype(jnp.int32).reshape(1)
        me = lax.axis_index("beta").astype(jnp.int32)

        sent = pack(start_vector, n_alpha)
        arrived = turn(sent)

        *marks, found = mark(source_blocks, me.reshape(1), n_beta, [sent])
        worst = marks[0][1:2, :1]
        marks = to_partners(marks)
        for other in marks:
            worst = jnp.maximum(worst, other[1:2, :1])
        too_many = worst[0, 0] > cap
        pairs_by_k = pair_index.T

        def plan(r):
            partner = (source_blocks // blocks) ^ me
            here = (found >= r * cap) & (found < (r + 1) * cap) & (partner != 0)
            far_slot = blocks + (partner - 1) * (cap + 1) + found - r * cap
            mine = (partner == 0) & (r == 0)
            slots = jnp.where(mine, source_blocks - me * blocks, jnp.where(here, far_slot, 0))
            signs = jnp.where(mine | here, phase_signs, 0)
            return positions(marks, r * cap, cap), slots.T, signs.T

        first_plan = plan(0)

        def beta_send(vector, planned, after):
            sent = gather_blocks(vector, planned[0], n_beta - 1, cap, after)
            received = to_partners(sent)
            return received, received[:2]

        def beta_round(vector, received, planned, after, dots=None, with_dot=False):
            _, slots, signs = planned
            return beta_sum(vector, received, slots, signs, pairs_by_k, pair_tables, after, dots, with_dot)

        def beta_side(vector, received, after, dots=None, with_dot=False):
            done = beta_round(vector, received, first_plan, after, dots, with_dot)

            def more(done):
                for r in range(1, -(-blocks // cap)):
                    planned = plan(r)
                    added = beta_round(vector, beta_send(vector, planned, [])[0], planned, [], None, with_dot)
                    done = [a + b for a, b in zip(done, added)]
                return done

            return lax.cond(too_many, more, lambda done: done, done)

        def alpha_side(arrived, with_dot, after):
            columns = arrived.reshape(n_alpha * rows, width)
            total = alpha_sum(columns, prepared, cross_pairs, cross_signs, device, after)
            dot = jnp.sum(columns * total, axis=0, keepdims=True) if with_dot else None
            return turn(total.reshape(n_alpha, rows, width)), dot, total

        received, token = beta_send(start_vector, first_plan, [])
        prepared = prepare(alpha_hamiltonian, alpha_pairs, pair_tables, [])
        returned, dot, _ = alpha_side(arrived, True, token)
        beta_term, sums = beta_side(start_vector, received, [], [dot], True)
        for other in to_partners([sums] * (n_beta - 1)):
            sums = sums + other
        sums = sums + lax.ppermute(sums, "alpha", [(i, i ^ 1) for i in range(n_alpha)])
        all_sums = [sums]
        for k in range(1, chips):
            pairs = [(i, ((i // 2 + k) % chips) * 2 + i % 2) for i in range(n_alpha)]
            all_sums.append(lax.ppermute(sums, "alpha", pairs))

        correction, parts = finish(returned, beta_term, (all_sums, start_vector, precondition))
        arrived = turn(parts)
        received, token = beta_send(correction, first_plan, [])
        returned, _, total = alpha_side(arrived, False, token)
        (beta_term,) = beta_side(correction, received, [total])
        (sigma_next,) = finish(returned, beta_term)
        return correction, sigma_next

    return local


def solution(mesh):
    placed = (
        P("alpha", "beta"),
        P("alpha", "beta"),
        P(),
        P(),
        P(),
        P("beta", None),
        P("beta", None),
        P("beta", None),
        P(None, "beta"),
        P(None, "beta"),
    )
    return jax.shard_map(
        make_local(mesh.shape["alpha"], mesh.shape["beta"]),
        mesh=mesh,
        in_specs=placed,
        out_specs=(P("alpha", "beta"), P("alpha", "beta")),
        check_vma=False,
    )
```

```python
import jax
import jax.numpy as jnp
from jax import lax
from jax.experimental import pallas as pl
from jax.experimental.pallas import tpu as pltpu
from jax.sharding import PartitionSpec as P

SB = 128
SHARE = 0.375
WORK = 20_000_000_000
VMEM_BYTES = 60 * 1024 * 1024
f32 = jnp.float32
bf16 = jnp.bfloat16


def params():
    return pltpu.CompilerParams(vmem_limit_bytes=VMEM_BYTES)


def divisor(number, most):
    return max(d for d in range(1, most + 1) if number % d == 0)


def halves(x):
    high = x.astype(bf16)
    return high, (x - high.astype(f32)).astype(bf16)


def mul(a, b):
    return jnp.dot(a, b, preferred_element_type=f32)


def cost(flops, count):
    return pl.CostEstimate(flops=max(flops, 1), bytes_accessed=max(count, 1), transcendentals=0)


def prepare(alpha_hamiltonian, alpha_pairs, pair_tables, after):
    size = alpha_hamiltonian.shape[0]
    nq = alpha_pairs.shape[0]
    depth = (nq + 1) * size
    npair = pair_tables.shape[0]

    def kernel(h_ref, p_ref, t_ref, *refs):
        a_twice, a_low, t_high, t_low = refs[-4:]
        for q in range(nq + 1):
            high, low = halves(h_ref[...] if q == 0 else p_ref[q - 1])
            a_twice[:, q * size : (q + 1) * size] = high
            a_twice[:, depth + q * size : depth + (q + 1) * size] = high
            a_low[:, q * size : (q + 1) * size] = low
        for p in range(npair):
            high, low = halves(t_ref[p])
            t_high[p, :SB, :] = high
            t_high[p, SB:, :] = high
            t_low[p] = low

    shapes = [(size, 2 * depth), (size, depth), (npair, 2 * SB, SB), (npair, SB, SB)]
    return pl.pallas_call(
        kernel,
        in_specs=[pl.BlockSpec(memory_space=pltpu.VMEM)] * 3 + [pl.BlockSpec(memory_space=pl.ANY)] * len(after),
        out_specs=[pl.BlockSpec(memory_space=pltpu.VMEM)] * 4,
        out_shape=[jax.ShapeDtypeStruct(shape, bf16) for shape in shapes],
        compiler_params=params(),
        cost_estimate=cost(0, 0),
        name="prepare",
    )(alpha_hamiltonian, alpha_pairs, pair_tables, *after)


def pack(vector, device, parts, wide, narrow):
    rows = vector.shape[0]

    def kernel(device_ref, source, *refs):
        targets = refs[: 1 + parts]
        held, few, sems = refs[-3:]
        copies = []
        for j in range(parts):
            copies.append((source.at[:, j * wide : (j + 1) * wide], held.at[j], targets[0].at[j]))
        for k in range(parts):
            at = pl.multiple_of(parts * wide + (device_ref[0] ^ k) * narrow, SB)
            copies.append((source.at[:, pl.ds(at, narrow)], few.at[k], targets[1 + k]))
        taken = [pltpu.make_async_copy(a, b, sems.at[0, i]) for i, (a, b, _) in enumerate(copies)]
        given = [pltpu.make_async_copy(b, c, sems.at[1, i]) for i, (_, b, c) in enumerate(copies)]
        for copy in taken:
            copy.start()
        for first, second in zip(taken, given):
            first.wait()
            second.start()
        for copy in given:
            copy.wait()

    anywhere = pl.BlockSpec(memory_space=pl.ANY)
    out = pl.pallas_call(
        kernel,
        in_specs=[pl.BlockSpec(memory_space=pltpu.SMEM), anywhere],
        out_specs=[anywhere] * (1 + parts),
        out_shape=[jax.ShapeDtypeStruct((parts, rows, wide), f32)]
        + [jax.ShapeDtypeStruct((rows, narrow), f32)] * parts,
        scratch_shapes=[
            pltpu.VMEM((parts, rows, wide), f32),
            pltpu.VMEM((parts, rows, narrow), f32),
            pltpu.SemaphoreType.DMA((2, 2 * parts)),
        ],
        compiler_params=params(),
        cost_estimate=cost(0, 0),
        name="pack",
    )(device, vector)
    return out[0], out[1:]


def alpha_sum(columns, prepared, cross_pairs, cross_signs, device, start, after, work, full, offset, previous):
    size, width = prepared[1].shape[0], columns[0].shape[1]
    count = len(columns)
    rows = size // count
    depth = prepared[1].shape[1]
    nq = cross_pairs.shape[0]
    blocks = width // SB
    per = divisor(blocks, 9)
    steps = blocks // per
    wide = per * SB

    def kernel(device_ref, pairs_ref, signs_ref, *refs):
        v_any = refs[:count]
        prepared_any = refs[count : count + 4]
        outs = refs[count + 4 + len(after) + len(previous) :][: 1 if full else count]
        v_held, out_held, a_twice, a_low, t_high, t_low, even, odd, sems, once = refs[-10:]

        def at(g):
            return pl.ds(pl.multiple_of(g * wide, SB), wide)

        def row(k):
            return pl.ds(pl.multiple_of((device_ref[0] ^ k) * rows, rows) if count > 1 else 0, rows)

        class Several:
            def __init__(self, copies):
                self.copies = copies

            def start(self):
                for copy in self.copies:
                    copy.start()

            def wait(self):
                for copy in self.copies:
                    copy.wait()

        def taken(g):
            return Several(
                [
                    pltpu.make_async_copy(v_any[k].at[:, at(g)], v_held.at[g, row(k)], sems.at[0, g, k])
                    for k in range(count)
                ]
            )

        def given(g):
            if full:
                to = pl.ds(offset + g * wide, wide)
                return pltpu.make_async_copy(out_held.at[g], outs[0].at[:, to], sems.at[1, g, 0])
            return Several(
                [
                    pltpu.make_async_copy(out_held.at[g, row(k)], outs[k].at[:, at(g)], sems.at[1, g, k])
                    for k in range(count)
                ]
            )

        held = (a_twice, a_low, t_high, t_low)
        loads = [pltpu.make_async_copy(prepared_any[i], held[i], once.at[i]) for i in range(4)]
        for load in loads[2:]:
            load.start()
        taken(0).start()
        for load in loads[:2]:
            load.start()
        for g in range(1, steps):
            taken(g).start()
        for load in loads[2:]:
            load.wait()

        def build(g, b):
            high, low = halves(v_held[g])
            b[:size, :] = high
            b[depth : depth + size, :] = low
            first = start + device_ref[0] * blocks + g * per
            for t in range(per):
                here = slice(t * SB, (t + 1) * SB)
                both = jnp.concatenate([high[:, here], low[:, here]], axis=1)
                chosen = [pairs_ref[q, first + t] for q in range(nq)]
                x = mul(both, jnp.concatenate([t_high[p] for p in chosen], axis=1))
                x = x + mul(high[:, here], jnp.concatenate([t_low[p] for p in chosen], axis=1))
                for q in range(nq):
                    x_high, x_low = halves(x[:, q * SB : (q + 1) * SB] * signs_ref[q, first + t].astype(f32))
                    row = (q + 1) * size
                    b[row : row + size, here] = x_high
                    b[depth + row : depth + row + size, here] = x_low

        taken(0).wait()
        build(0, even)
        for load in loads[:2]:
            load.wait()
        for g in range(steps):
            b, other = (even, odd) if g % 2 == 0 else (odd, even)
            if g + 1 < steps:
                taken(g + 1).wait()
                build(g + 1, other)
            out_held[g] = mul(a_twice[...], b[...]) + mul(a_low[...], b[:depth, :])
            given(g).start()
        for g in range(steps):
            given(g).wait()

    anywhere = pl.BlockSpec(memory_space=pl.ANY)
    return pl.pallas_call(
        kernel,
        in_specs=[pl.BlockSpec(memory_space=pltpu.SMEM)] * 3 + [anywhere] * (count + 4 + len(after) + len(previous)),
        out_specs=[anywhere] * (1 if full else count),
        out_shape=[jax.ShapeDtypeStruct((size, full), f32)]
        if full
        else [jax.ShapeDtypeStruct((rows, width), f32)] * count,
        input_output_aliases={3 + count + 4 + len(after): 0} if previous else {},
        scratch_shapes=[pltpu.VMEM((steps, size, wide), f32)] * 2
        + [pltpu.VMEM(a.shape, bf16) for a in prepared]
        + [
            pltpu.VMEM((2 * depth, wide), bf16),
            pltpu.VMEM((2 * depth, wide), bf16),
            pltpu.SemaphoreType.DMA((2, steps, count)),
            pltpu.SemaphoreType.DMA((4,)),
        ],
        compiler_params=params(),
        cost_estimate=cost(work, work // 300),
        name="alpha_sum",
    )(device, cross_pairs, cross_signs, *columns, *prepared, *after, *previous)


def earlier(lanes):
    row = lax.broadcasted_iota(jnp.int32, (lanes, lanes), 0)
    column = lax.broadcasted_iota(jnp.int32, (lanes, lanes), 1)
    return jnp.where(row < column, 1.0, 0.0).astype(bf16)


def mark(source_blocks, me, parts, after):
    blocks, kb = source_blocks.shape
    lanes = -(-blocks // SB) * SB
    tall = -(-parts // 8) * 8

    def kernel(me_ref, source_ref, *refs):
        marks_refs = refs[len(after) : len(after) + parts - 1]
        found_ref, held = refs[-2:]
        lane = lax.broadcasted_iota(jnp.int32, (blocks, lanes), 1)

        def hit(s, k):
            return (source_ref[:, k : k + 1] - s * blocks == lane) & (lane < blocks)

        held[...] = jnp.zeros_like(held)
        worst = jnp.zeros((1, 1), f32)
        for s in range(parts):
            needed = jnp.zeros((1, lanes), f32)
            for k in range(kb):
                needed = jnp.maximum(needed, jnp.max(jnp.where(hit(s, k), 1.0, 0.0), axis=0, keepdims=True))
            held[s : s + 1, :] = needed
            count = jnp.sum(needed, axis=1, keepdims=True)
            worst = jnp.maximum(worst, jnp.where(me_ref[0] == s, 0.0, count))
        place = mul(held[...].astype(bf16), earlier(lanes))
        for k in range(kb):
            found = jnp.zeros((blocks, 1), f32)
            for s in range(parts):
                found = found + jnp.sum(jnp.where(hit(s, k), place[s : s + 1, :], 0.0), axis=1, keepdims=True)
            found_ref[:, k : k + 1] = found.astype(jnp.int32)
        for k, marks_ref in enumerate(marks_refs, 1):
            marks_ref[...] = jnp.zeros_like(marks_ref)
            marks_ref[0:1, :] = held[pl.ds(me_ref[0] ^ k, 1), :]
            marks_ref[1:2, :] = jnp.broadcast_to(worst, (1, lanes))

    return pl.pallas_call(
        kernel,
        in_specs=[pl.BlockSpec(memory_space=pltpu.SMEM), pl.BlockSpec(memory_space=pltpu.VMEM)]
        + [pl.BlockSpec(memory_space=pl.ANY)] * len(after),
        out_specs=[pl.BlockSpec(memory_space=pltpu.VMEM)] * parts,
        out_shape=[jax.ShapeDtypeStruct((8, lanes), f32)] * (parts - 1)
        + [jax.ShapeDtypeStruct((blocks, kb), jnp.int32)],
        scratch_shapes=[pltpu.VMEM((tall, lanes), f32)],
        compiler_params=params(),
        cost_estimate=cost(0, 0),
        name="mark",
    )(me, source_blocks, *after)


def positions(marks, first, cap):
    lanes = marks[0].shape[1]
    count = len(marks)
    tall = -(-count // 8) * 8

    def kernel(*refs):
        out_ref, held = refs[-2:]
        held[...] = jnp.zeros_like(held)
        for k in range(count):
            held[k : k + 1, :] = refs[k][0:1, :]
        needed = held[...]
        slot = mul(needed.astype(bf16), earlier(lanes)).astype(jnp.int32) - first
        out_ref[...] = jnp.where((needed > 0) & (slot >= 0) & (slot < cap), slot, cap)

    return pl.pallas_call(
        kernel,
        in_specs=[pl.BlockSpec(memory_space=pltpu.VMEM)] * count,
        out_specs=pl.BlockSpec(memory_space=pltpu.VMEM),
        out_shape=jax.ShapeDtypeStruct((tall, lanes), jnp.int32),
        scratch_shapes=[pltpu.VMEM((tall, lanes), f32)],
        compiler_params=params(),
        cost_estimate=cost(0, 0),
        name="positions",
    )(*marks)


def gather_blocks(vector, slots, count, cap, after):
    rows, cols = vector.shape

    def kernel(slots_ref, v_ref, *refs):
        outs = refs[len(after) :]

        @pl.loop(0, cols // SB, unroll=4)
        def _(b):
            block = v_ref[:, pl.ds(pl.multiple_of(b * SB, SB), SB)]
            for k in range(count):
                outs[k][slots_ref[k, b]] = block

    shape = (cap + 1, rows, SB)
    return pl.pallas_call(
        kernel,
        grid_spec=pltpu.PrefetchScalarGridSpec(
            num_scalar_prefetch=1,
            grid=(1,),
            in_specs=[pl.BlockSpec(vector.shape, lambda g, *_: (0, 0))]
            + [pl.BlockSpec(memory_space=pl.ANY)] * len(after),
            out_specs=[pl.BlockSpec(shape, lambda g, *_: (0, 0, 0))] * count,
        ),
        out_shape=[jax.ShapeDtypeStruct(shape, f32)] * count,
        compiler_params=params(),
        cost_estimate=cost(0, 0),
        name="gather_blocks",
    )(slots, vector, *after)


def beta_sum(vector, received, slots, signs, pair_index, pair_tables, after, dots=None, with_dot=False, work=0):
    rows, cols = vector.shape
    blocks = cols // SB
    npair = pair_tables.shape[0]
    kb = slots.shape[0]
    far = len(received)
    each = received[0].shape[0]
    dots = [] if dots is None else dots
    per = divisor(blocks, 16)
    steps = blocks // per

    def kernel(slots_ref, sign_ref, pair_ref, *refs):
        v_ref, t_ref = refs[:2]
        r_refs = refs[2 : 2 + far]
        at = 2 + far + len(after)
        dot_refs = refs[at : at + len(dots)]
        out_ref = refs[at + len(dots)]
        pool, wide, t_high, t_low, sems = refs[-5:]
        g = pl.program_id(0)

        @pl.when(g == 0)
        def _():
            copies = [
                pltpu.make_async_copy(r_refs[i], pool.at[pl.ds(i * each, each)], sems.at[i]) for i in range(far)
            ]
            for copy in copies:
                copy.start()
            for p in range(npair):
                high, low = halves(t_ref[p])
                t_high[p * SB : (p + 1) * SB, :] = high
                t_low[p * SB : (p + 1) * SB, :] = low
            for copy in copies:
                copy.wait()

        wide[...] = jnp.zeros_like(wide)
        for t in range(per):
            target = g * per + t
            for k in range(kb):
                slot = slots_ref[k, target]
                own = v_ref[:, pl.ds(pl.multiple_of(lax.min(slot, blocks - 1) * SB, SB), SB)]
                other = pool[lax.max(slot - blocks, 0)]
                block = jnp.where(slot < blocks, own, other) * sign_ref[k, target].astype(f32)
                at = pl.ds(pl.multiple_of(pair_ref[k, target] * SB, SB), SB)
                wide[t * rows : (t + 1) * rows, at] += block
        high, low = halves(wide[...])
        total = mul(high, t_high[...]) + mul(low, t_high[...]) + mul(high, t_low[...])
        for t in range(per):
            out_ref[:, t * SB : (t + 1) * SB] = total[t * rows : (t + 1) * rows]
        if with_dot:
            sums_ref = refs[-6]
            dot = jnp.zeros((rows, SB), f32)
            square = jnp.zeros((rows, SB), f32)
            for t in range(per):
                v = v_ref[:, pl.ds(pl.multiple_of((g * per + t) * SB, SB), SB)]
                dot = dot + total[t * rows : (t + 1) * rows] * v
                square = square + v * v
            dot = jnp.sum(dot, axis=0, keepdims=True)
            square = jnp.sum(square, axis=0, keepdims=True)

            @pl.when(g == 0)
            def _():
                sums_ref[...] = jnp.zeros_like(sums_ref)

            sums_ref[0:1, :] += dot
            if dots:
                sums_ref[1:2, :] += square

            @pl.when(g == steps - 1)
            def _():
                value = sums_ref[...]
                for ref in dot_refs:
                    for at in range(0, ref.shape[1], SB):
                        first = lax.broadcasted_iota(jnp.int32, value.shape, 0) == 0
                        value = value + jnp.where(first, ref[:, at : at + SB], 0.0)
                sums_ref[...] = value

    out = pl.pallas_call(
        kernel,
        grid_spec=pltpu.PrefetchScalarGridSpec(
            num_scalar_prefetch=3,
            grid=(steps,),
            in_specs=[
                pl.BlockSpec((rows, cols), lambda g, *_: (0, 0)),
                pl.BlockSpec(pair_tables.shape, lambda g, *_: (0, 0, 0)),
            ]
            + [pl.BlockSpec(memory_space=pl.ANY)] * (far + len(after))
            + [pl.BlockSpec(dot.shape, lambda g, *_: (0, 0)) for dot in dots],
            out_specs=[pl.BlockSpec((rows, per * SB), lambda g, *_: (0, g))]
            + ([pl.BlockSpec((8, SB), lambda g, *_: (0, 0))] if with_dot else []),
            scratch_shapes=[
                pltpu.VMEM((far * each, rows, SB), f32),
                pltpu.VMEM((per * rows, npair * SB), f32),
                pltpu.VMEM((npair * SB, SB), bf16),
                pltpu.VMEM((npair * SB, SB), bf16),
                pltpu.SemaphoreType.DMA((far,)),
            ],
        ),
        out_shape=[jax.ShapeDtypeStruct((rows, cols), f32)]
        + ([jax.ShapeDtypeStruct((8, SB), f32)] if with_dot else []),
        compiler_params=params(),
        cost_estimate=cost(work, work // 300),
        name="beta_sum",
    )(slots, signs, pair_index, vector, pair_tables, *received, *after, *dots)
    return list(out)


def correct(returned, beta_term, device, wide, narrow, extra):
    rows, cols = beta_term.shape
    parts = returned.shape[0]
    sums = [] if extra is None else extra[0]
    wholes = [beta_term] + ([] if extra is None else [extra[1], extra[2]])
    count = len(wholes)
    sent = 0 if extra is None else 1 + parts

    def kernel(device_ref, *refs):
        sum_refs = refs[: len(sums)]
        whole_refs = refs[len(sums) :][:count]
        part_ref = refs[len(sums) + count]
        out_refs = refs[len(sums) + count + 1 :][: 1 + sent]
        held, few, sems, out_sems = refs[-4:]
        pieces = []
        for j in range(parts):
            pieces.append((held, j, j * wide, part_ref.at[j, :, :wide], out_refs[1].at[j] if sent else None))
        for k in range(parts):
            place = device_ref[0] ^ k
            at = pl.multiple_of(parts * wide + place * narrow, SB)
            pieces.append((few, k, at, part_ref.at[place, :, wide:], out_refs[2 + k] if sent else None))
        taken = []
        given = []
        for p, (buffer, j, start, part, target) in enumerate(pieces):
            at = pl.ds(start, buffer.shape[-1])
            taken.append(
                [pltpu.make_async_copy(whole_refs[i].at[:, at], buffer.at[i, j], sems.at[i, p]) for i in range(count)]
                + [pltpu.make_async_copy(part, buffer.at[count, j], sems.at[count, p])]
            )
            given.append([pltpu.make_async_copy(buffer.at[count, j], out_refs[0].at[:, at], out_sems.at[0, p])])
            if sent:
                given[-1].append(pltpu.make_async_copy(buffer.at[count, j], target, out_sems.at[1, p]))
        for copies in taken:
            for copy in copies:
                copy.start()
        if extra is not None:
            total = sum_refs[0][...]
            for ref in sum_refs[1:]:
                total = total + ref[...]
            both = [jnp.sum(total[i : i + 1], axis=1, keepdims=True) for i in range(2)]
            theta = both[0] / both[1]
        for p, (buffer, j, _, _, _) in enumerate(pieces):
            for copy in taken[p]:
                copy.wait()
            value = buffer[0, j] + buffer[count, j]
            if extra is not None:
                value = (value - theta * buffer[1, j]) / buffer[2, j]
            buffer[count, j] = value
            for copy in given[p]:
                copy.start()
        for copies in given:
            for copy in copies:
                copy.wait()

    anywhere = pl.BlockSpec(memory_space=pl.ANY)
    shapes = [(rows, cols), (parts, rows, wide)] + [(rows, narrow)] * parts
    out = pl.pallas_call(
        kernel,
        in_specs=[pl.BlockSpec(memory_space=pltpu.SMEM)]
        + [pl.BlockSpec(memory_space=pltpu.VMEM)] * len(sums)
        + [anywhere] * (count + 1),
        out_specs=[anywhere] * (1 + sent),
        out_shape=[jax.ShapeDtypeStruct(shape, f32) for shape in shapes[: 1 + sent]],
        scratch_shapes=[
            pltpu.VMEM((count + 1, parts, rows, wide), f32),
            pltpu.VMEM((count + 1, parts, rows, narrow), f32),
            pltpu.SemaphoreType.DMA((count + 1, 2 * parts)),
            pltpu.SemaphoreType.DMA((2, 2 * parts)),
        ],
        compiler_params=params(),
        cost_estimate=cost(0, 0),
        name="finish" if extra is None else "correct",
    )(device, *sums, *wholes, returned)
    return out if extra is not None else out[0]


def finish(returned, beta_term, device, start, previous, extra=None, work=0):
    rows, cols = beta_term.shape
    listed = isinstance(returned, (list, tuple))
    arrays = list(returned) if listed else [returned]
    parts = len(arrays) if listed else returned.shape[0]
    width = arrays[0].shape[-1]
    sums = [] if extra is None else extra[0]
    wholes = [beta_term] + ([] if extra is None else [extra[1], extra[2]])
    count = len(wholes)
    aliased = [] if previous is None else [previous]
    sent = [] if extra is None else arrays

    def kernel(device_ref, *refs):
        sum_refs = refs[: len(sums)]
        whole_refs = refs[len(sums) :][:count]
        part_refs = refs[len(sums) + count :][: len(arrays)]
        out_refs = refs[len(sums) + count + len(arrays) + len(aliased) :][: 1 + len(sent)]
        held, sems, out_sems = refs[-3:]

        def piece(among, j):
            return among[j] if listed else among[0].at[j]

        taken = []
        given = []
        for j in range(parts):
            place = device_ref[0] ^ j if listed else j
            at = pl.ds(pl.multiple_of(start + place * width, SB), width)
            taken.append(
                [pltpu.make_async_copy(whole_refs[i].at[:, at], held.at[i, j], sems.at[i, j]) for i in range(count)]
                + [pltpu.make_async_copy(piece(part_refs, j), held.at[count, j], sems.at[count, j])]
            )
            given.append([pltpu.make_async_copy(held.at[count, j], out_refs[0].at[:, at], out_sems.at[0, j])])
            if sent:
                target = piece(out_refs[1:], j)
                given[-1].append(pltpu.make_async_copy(held.at[count, j], target, out_sems.at[1, j]))
        for copies in taken:
            for copy in copies:
                copy.start()
        if extra is not None:
            total = sum_refs[0][...]
            for ref in sum_refs[1:]:
                total = total + ref[...]
            both = [jnp.sum(total[i : i + 1], axis=1, keepdims=True) for i in range(2)]
            theta = both[0] / both[1]
        for j in range(parts):
            for copy in taken[j]:
                copy.wait()
            value = held[0, j] + held[count, j]
            if extra is not None:
                value = (value - theta * held[1, j]) / held[2, j]
            held[count, j] = value
            for copy in given[j]:
                copy.start()
        for copies in given:
            for copy in copies:
                copy.wait()

    anywhere = pl.BlockSpec(memory_space=pl.ANY)
    out = pl.pallas_call(
        kernel,
        in_specs=[pl.BlockSpec(memory_space=pltpu.SMEM)]
        + [pl.BlockSpec(memory_space=pltpu.VMEM)] * len(sums)
        + [anywhere] * (count + len(arrays) + len(aliased)),
        out_specs=[anywhere] * (1 + len(sent)),
        out_shape=[jax.ShapeDtypeStruct(a.shape, f32) for a in [beta_term] + sent],
        input_output_aliases={1 + len(sums) + count + len(arrays): 0} if aliased else {},
        scratch_shapes=[
            pltpu.VMEM((count + 1, parts, rows, width), f32),
            pltpu.SemaphoreType.DMA((count + 1, parts)),
            pltpu.SemaphoreType.DMA((2, parts)),
        ],
        compiler_params=params(),
        cost_estimate=cost(work, work // 300),
        name="finish" if extra is None else "correct",
    )(device, *sums, *wholes, *arrays, *aliased)
    return out[0], out[1:]


def make_local(n_alpha, n_beta):
    chips = n_alpha // 2

    def to_partners(parts):
        return [lax.ppermute(part, "beta", [(i, i ^ k) for i in range(n_beta)]) for k, part in enumerate(parts, 1)]

    def turn(parts):
        return lax.all_to_all(parts, "alpha", 0, 0, tiled=True)

    def swap(parts):
        moved = list(parts)
        for k in range(n_alpha - 1, 0, -1):
            moved[k] = lax.ppermute(parts[k], "alpha", [(i, i ^ k) for i in range(n_alpha)])
        return moved

    def local(
        start_vector,
        precondition,
        alpha_hamiltonian,
        alpha_pairs,
        pair_tables,
        source_blocks,
        pair_index,
        phase_signs,
        cross_pairs,
        cross_signs,
    ):
        rows, cols = start_vector.shape
        blocks = cols // SB
        mine = blocks // n_alpha
        few = max(1, round(mine * SHARE))
        wide, narrow = (mine - few) * SB, few * SB
        border = n_alpha * wide
        cap = (blocks + 1) // 2
        device = lax.axis_index("alpha").astype(jnp.int32).reshape(1)
        me = lax.axis_index("beta").astype(jnp.int32)

        sent, sent_few = pack(start_vector, device, n_alpha, wide, narrow)
        arrived = turn(sent)
        arrived_few = swap(sent_few)

        *marks, found = mark(source_blocks, me.reshape(1), n_beta, [sent])
        worst = marks[0][1:2, :1]
        marks = to_partners(marks)
        for other in marks:
            worst = jnp.maximum(worst, other[1:2, :1])
        too_many = worst[0, 0] > cap
        pairs_by_k = pair_index.T

        def plan(r):
            partner = (source_blocks // blocks) ^ me
            here = (found >= r * cap) & (found < (r + 1) * cap) & (partner != 0)
            far_slot = blocks + (partner - 1) * (cap + 1) + found - r * cap
            mine = (partner == 0) & (r == 0)
            slots = jnp.where(mine, source_blocks - me * blocks, jnp.where(here, far_slot, 0))
            signs = jnp.where(mine | here, phase_signs, 0)
            return positions(marks, r * cap, cap), slots.T, signs.T

        first_plan = plan(0)

        def beta_send(vector, planned, after):
            sent = gather_blocks(vector, planned[0], n_beta - 1, cap, after)
            received = to_partners(sent)
            return received, (received[:2], received[2:])

        def beta_round(vector, received, planned, after, dots=None, with_dot=False, work=0):
            _, slots, signs = planned
            return beta_sum(vector, received, slots, signs, pairs_by_k, pair_tables, after, dots, with_dot, work)

        def beta_side(vector, received, after, dots=None, with_dot=False, work=0):
            done = beta_round(vector, received, first_plan, after, dots, with_dot, work)

            def more(done):
                for r in range(1, -(-blocks // cap)):
                    planned = plan(r)
                    added = beta_round(vector, beta_send(vector, planned, [])[0], planned, [], None, with_dot)
                    done = [a + b for a, b in zip(done, added)]
                return done

            return lax.cond(too_many, more, lambda done: done, done)

        received, token = beta_send(start_vector, first_plan, [])
        prepared = prepare(alpha_hamiltonian, alpha_pairs, pair_tables, [])
        common = (prepared, cross_pairs, cross_signs, device)
        width = wide + narrow
        columns = arrived.reshape(n_alpha * rows, wide)
        first = alpha_sum([columns], *common, 0, token[0], WORK, width, 0, [])
        (total,) = alpha_sum(arrived_few, *common, border // SB, [], 0, width, wide, first)
        returned = turn(total.reshape(n_alpha, rows, width))
        dots = [jnp.sum(columns * total[:, :wide], axis=0, keepdims=True)]
        last = total[:, wide:].reshape(n_alpha, rows, narrow)
        few = [lax.dynamic_index_in_dim(last, device[0] ^ k, 0, keepdims=False) for k in range(n_alpha)]
        dots.append(sum(jnp.sum(a * b, axis=0, keepdims=True) for a, b in zip(arrived_few, few)))
        beta_term, sums = beta_side(start_vector, received, [], dots, True)
        for other in to_partners([sums] * (n_beta - 1)):
            sums = sums + other
        sums = sums + lax.ppermute(sums, "alpha", [(i, i ^ 1) for i in range(n_alpha)])
        all_sums = [sums]
        for k in range(1, chips):
            pairs = [(i, ((i // 2 + k) % chips) * 2 + i % 2) for i in range(n_alpha)]
            all_sums.append(lax.ppermute(sums, "alpha", pairs))

        extra = (all_sums, start_vector, precondition)
        correction, parts, *few = correct(returned, beta_term, device, wide, narrow, extra)
        arrived = turn(parts)
        arrived_few = swap(few)
        received, token = beta_send(correction, first_plan, [])
        columns = arrived.reshape(n_alpha * rows, wide)
        (total,) = alpha_sum([columns], *common, 0, token[0], WORK, wide, 0, [])
        returned = turn(total.reshape(n_alpha, rows, wide))
        totals = alpha_sum(arrived_few, *common, border // SB, [total, *token[1]], 10 * WORK, 0, 0, [])
        returned_few = swap(totals)
        (beta_term,) = beta_side(correction, received, totals[:1], work=WORK)
        sigma_next, _ = finish(returned, beta_term, device, 0, None, None, WORK)
        sigma_next, _ = finish(returned_few, beta_term, device, border, sigma_next)
        return correction, sigma_next

    return local


def solution(mesh):
    placed = (
        P("alpha", "beta"),
        P("alpha", "beta"),
        P(),
        P(),
        P(),
        P("beta", None),
        P("beta", None),
        P("beta", None),
        P(None, "beta"),
        P(None, "beta"),
    )
    return jax.shard_map(
        make_local(mesh.shape["alpha"], mesh.shape["beta"]),
        mesh=mesh,
        in_specs=placed,
        out_specs=(P("alpha", "beta"), P("alpha", "beta")),
        check_vma=False,
    )
```

```python
import jax
import jax.numpy as jnp
from jax import lax
from jax.experimental import pallas as pl
from jax.experimental.pallas import tpu as pltpu
from jax.sharding import PartitionSpec as P

SB = 128
SHARE = 0.375
WORK = 20_000_000_000
VMEM_BYTES = 60 * 1024 * 1024
f32 = jnp.float32
bf16 = jnp.bfloat16


def params():
    return pltpu.CompilerParams(vmem_limit_bytes=VMEM_BYTES)


def divisor(number, most):
    return max(d for d in range(1, most + 1) if number % d == 0)


def halves(x):
    high = x.astype(bf16)
    return high, (x - high.astype(f32)).astype(bf16)


def mul(a, b):
    return jnp.dot(a, b, preferred_element_type=f32)


def cost(flops, count):
    return pl.CostEstimate(flops=max(flops, 1), bytes_accessed=max(count, 1), transcendentals=0)


def prepare(alpha_hamiltonian, alpha_pairs, pair_tables, after):
    size = alpha_hamiltonian.shape[0]
    nq = alpha_pairs.shape[0]
    depth = (nq + 1) * size
    npair = pair_tables.shape[0]

    def kernel(h_ref, p_ref, t_ref, *refs):
        a_twice, a_low, t_high, t_low = refs[-4:]
        for q in range(nq + 1):
            high, low = halves(h_ref[...] if q == 0 else p_ref[q - 1])
            a_twice[:, q * size : (q + 1) * size] = high
            a_twice[:, depth + q * size : depth + (q + 1) * size] = high
            a_low[:, q * size : (q + 1) * size] = low
        for p in range(npair):
            high, low = halves(t_ref[p])
            t_high[p, :SB, :] = high
            t_high[p, SB:, :] = high
            t_low[p] = low

    shapes = [(size, 2 * depth), (size, depth), (npair, 2 * SB, SB), (npair, SB, SB)]
    return pl.pallas_call(
        kernel,
        in_specs=[pl.BlockSpec(memory_space=pltpu.VMEM)] * 3 + [pl.BlockSpec(memory_space=pl.ANY)] * len(after),
        out_specs=[pl.BlockSpec(memory_space=pltpu.VMEM)] * 4,
        out_shape=[jax.ShapeDtypeStruct(shape, bf16) for shape in shapes],
        compiler_params=params(),
        cost_estimate=cost(0, 0),
        name="prepare",
    )(alpha_hamiltonian, alpha_pairs, pair_tables, *after)


def pack(vector, device, parts, wide, narrow):
    rows = vector.shape[0]

    def kernel(device_ref, source, *refs):
        targets = refs[: 1 + parts]
        held, few, sems = refs[-3:]
        copies = []
        for j in range(parts):
            copies.append((source.at[:, j * wide : (j + 1) * wide], held.at[j], targets[0].at[j]))
        for k in range(parts):
            at = pl.multiple_of(parts * wide + (device_ref[0] ^ k) * narrow, SB)
            copies.append((source.at[:, pl.ds(at, narrow)], few.at[k], targets[1 + k]))
        taken = [pltpu.make_async_copy(a, b, sems.at[0, i]) for i, (a, b, _) in enumerate(copies)]
        given = [pltpu.make_async_copy(b, c, sems.at[1, i]) for i, (_, b, c) in enumerate(copies)]
        for copy in taken:
            copy.start()
        for first, second in zip(taken, given):
            first.wait()
            second.start()
        for copy in given:
            copy.wait()

    anywhere = pl.BlockSpec(memory_space=pl.ANY)
    out = pl.pallas_call(
        kernel,
        in_specs=[pl.BlockSpec(memory_space=pltpu.SMEM), anywhere],
        out_specs=[anywhere] * (1 + parts),
        out_shape=[jax.ShapeDtypeStruct((parts, rows, wide), f32)]
        + [jax.ShapeDtypeStruct((rows, narrow), f32)] * parts,
        scratch_shapes=[
            pltpu.VMEM((parts, rows, wide), f32),
            pltpu.VMEM((parts, rows, narrow), f32),
            pltpu.SemaphoreType.DMA((2, 2 * parts)),
        ],
        compiler_params=params(),
        cost_estimate=cost(0, 0),
        name="pack",
    )(device, vector)
    return out[0], out[1:]


def alpha_sum(columns, prepared, cross_pairs, cross_signs, device, start, after, work, full, offset, previous):
    size, width = prepared[1].shape[0], columns[0].shape[1]
    count = len(columns)
    rows = size // count
    depth = prepared[1].shape[1]
    nq = cross_pairs.shape[0]
    blocks = width // SB
    per = divisor(blocks, 9)
    steps = blocks // per
    wide = per * SB

    def kernel(device_ref, pairs_ref, signs_ref, *refs):
        v_any = refs[:count]
        prepared_any = refs[count : count + 4]
        outs = refs[count + 4 + len(after) + len(previous) :][: 1 if full else count]
        v_held, out_held, a_twice, a_low, t_high, t_low, even, odd, sems, once = refs[-10:]

        def at(g):
            return pl.ds(pl.multiple_of(g * wide, SB), wide)

        def row(k):
            return pl.ds(pl.multiple_of((device_ref[0] ^ k) * rows, rows) if count > 1 else 0, rows)

        class Several:
            def __init__(self, copies):
                self.copies = copies

            def start(self):
                for copy in self.copies:
                    copy.start()

            def wait(self):
                for copy in self.copies:
                    copy.wait()

        def taken(g):
            return Several(
                [
                    pltpu.make_async_copy(v_any[k].at[:, at(g)], v_held.at[g, row(k)], sems.at[0, g, k])
                    for k in range(count)
                ]
            )

        def given(g):
            if full:
                to = pl.ds(offset + g * wide, wide)
                return pltpu.make_async_copy(out_held.at[g], outs[0].at[:, to], sems.at[1, g, 0])
            return Several(
                [
                    pltpu.make_async_copy(out_held.at[g, row(k)], outs[k].at[:, at(g)], sems.at[1, g, k])
                    for k in range(count)
                ]
            )

        held = (a_twice, a_low, t_high, t_low)
        loads = [pltpu.make_async_copy(prepared_any[i], held[i], once.at[i]) for i in range(4)]
        for load in loads[2:]:
            load.start()
        taken(0).start()
        for load in loads[:2]:
            load.start()
        for g in range(1, steps):
            taken(g).start()
        for load in loads[2:]:
            load.wait()

        def build(g, b):
            high, low = halves(v_held[g])
            b[:size, :] = high
            b[depth : depth + size, :] = low
            first = start + device_ref[0] * blocks + g * per
            for t in range(per):
                here = slice(t * SB, (t + 1) * SB)
                both = jnp.concatenate([high[:, here], low[:, here]], axis=1)
                chosen = [pairs_ref[q, first + t] for q in range(nq)]
                x = mul(both, jnp.concatenate([t_high[p] for p in chosen], axis=1))
                x = x + mul(high[:, here], jnp.concatenate([t_low[p] for p in chosen], axis=1))
                for q in range(nq):
                    x_high, x_low = halves(x[:, q * SB : (q + 1) * SB] * signs_ref[q, first + t].astype(f32))
                    row = (q + 1) * size
                    b[row : row + size, here] = x_high
                    b[depth + row : depth + row + size, here] = x_low

        taken(0).wait()
        build(0, even)
        for load in loads[:2]:
            load.wait()
        for g in range(steps):
            b, other = (even, odd) if g % 2 == 0 else (odd, even)
            if g + 1 < steps:
                taken(g + 1).wait()
                build(g + 1, other)
            out_held[g] = mul(a_twice[...], b[...]) + mul(a_low[...], b[:depth, :])
            given(g).start()
        for g in range(steps):
            given(g).wait()

    anywhere = pl.BlockSpec(memory_space=pl.ANY)
    return pl.pallas_call(
        kernel,
        in_specs=[pl.BlockSpec(memory_space=pltpu.SMEM)] * 3 + [anywhere] * (count + 4 + len(after) + len(previous)),
        out_specs=[anywhere] * (1 if full else count),
        out_shape=[jax.ShapeDtypeStruct((size, full), f32)]
        if full
        else [jax.ShapeDtypeStruct((rows, width), f32)] * count,
        input_output_aliases={3 + count + 4 + len(after): 0} if previous else {},
        scratch_shapes=[pltpu.VMEM((steps, size, wide), f32)] * 2
        + [pltpu.VMEM(a.shape, bf16) for a in prepared]
        + [
            pltpu.VMEM((2 * depth, wide), bf16),
            pltpu.VMEM((2 * depth, wide), bf16),
            pltpu.SemaphoreType.DMA((2, steps, count)),
            pltpu.SemaphoreType.DMA((4,)),
        ],
        compiler_params=params(),
        cost_estimate=cost(work, work // 300),
        name="alpha_sum",
    )(device, cross_pairs, cross_signs, *columns, *prepared, *after, *previous)


def earlier(lanes):
    row = lax.broadcasted_iota(jnp.int32, (lanes, lanes), 0)
    column = lax.broadcasted_iota(jnp.int32, (lanes, lanes), 1)
    return jnp.where(row < column, 1.0, 0.0).astype(bf16)


def mark(source_blocks, me, parts, after):
    blocks, kb = source_blocks.shape
    lanes = -(-blocks // SB) * SB
    tall = -(-parts // 8) * 8

    def kernel(me_ref, source_ref, *refs):
        marks_refs = refs[len(after) : len(after) + parts - 1]
        found_ref, held = refs[-2:]
        lane = lax.broadcasted_iota(jnp.int32, (blocks, lanes), 1)

        def hit(s, k):
            return (source_ref[:, k : k + 1] - s * blocks == lane) & (lane < blocks)

        held[...] = jnp.zeros_like(held)
        worst = jnp.zeros((1, 1), f32)
        for s in range(parts):
            needed = jnp.zeros((1, lanes), f32)
            for k in range(kb):
                needed = jnp.maximum(needed, jnp.max(jnp.where(hit(s, k), 1.0, 0.0), axis=0, keepdims=True))
            held[s : s + 1, :] = needed
            count = jnp.sum(needed, axis=1, keepdims=True)
            worst = jnp.maximum(worst, jnp.where(me_ref[0] == s, 0.0, count))
        place = mul(held[...].astype(bf16), earlier(lanes))
        for k in range(kb):
            found = jnp.zeros((blocks, 1), f32)
            for s in range(parts):
                found = found + jnp.sum(jnp.where(hit(s, k), place[s : s + 1, :], 0.0), axis=1, keepdims=True)
            found_ref[:, k : k + 1] = found.astype(jnp.int32)
        for k, marks_ref in enumerate(marks_refs, 1):
            marks_ref[...] = jnp.zeros_like(marks_ref)
            marks_ref[0:1, :] = held[pl.ds(me_ref[0] ^ k, 1), :]
            marks_ref[1:2, :] = jnp.broadcast_to(worst, (1, lanes))

    return pl.pallas_call(
        kernel,
        in_specs=[pl.BlockSpec(memory_space=pltpu.SMEM), pl.BlockSpec(memory_space=pltpu.VMEM)]
        + [pl.BlockSpec(memory_space=pl.ANY)] * len(after),
        out_specs=[pl.BlockSpec(memory_space=pltpu.VMEM)] * parts,
        out_shape=[jax.ShapeDtypeStruct((8, lanes), f32)] * (parts - 1)
        + [jax.ShapeDtypeStruct((blocks, kb), jnp.int32)],
        scratch_shapes=[pltpu.VMEM((tall, lanes), f32)],
        compiler_params=params(),
        cost_estimate=cost(0, 0),
        name="mark",
    )(me, source_blocks, *after)


def positions(marks, first, cap):
    lanes = marks[0].shape[1]
    count = len(marks)
    tall = -(-count // 8) * 8

    def kernel(*refs):
        out_ref, held = refs[-2:]
        held[...] = jnp.zeros_like(held)
        for k in range(count):
            held[k : k + 1, :] = refs[k][0:1, :]
        needed = held[...]
        slot = mul(needed.astype(bf16), earlier(lanes)).astype(jnp.int32) - first
        out_ref[...] = jnp.where((needed > 0) & (slot >= 0) & (slot < cap), slot, cap)

    return pl.pallas_call(
        kernel,
        in_specs=[pl.BlockSpec(memory_space=pltpu.VMEM)] * count,
        out_specs=pl.BlockSpec(memory_space=pltpu.VMEM),
        out_shape=jax.ShapeDtypeStruct((tall, lanes), jnp.int32),
        scratch_shapes=[pltpu.VMEM((tall, lanes), f32)],
        compiler_params=params(),
        cost_estimate=cost(0, 0),
        name="positions",
    )(*marks)


def gather_blocks(vector, slots, count, cap, after):
    rows, cols = vector.shape

    def kernel(slots_ref, v_ref, *refs):
        outs = refs[len(after) :]

        @pl.loop(0, cols // SB, unroll=4)
        def _(b):
            block = v_ref[:, pl.ds(pl.multiple_of(b * SB, SB), SB)]
            for k in range(count):
                outs[k][slots_ref[k, b]] = block

    shape = (cap + 1, rows, SB)
    return pl.pallas_call(
        kernel,
        grid_spec=pltpu.PrefetchScalarGridSpec(
            num_scalar_prefetch=1,
            grid=(1,),
            in_specs=[pl.BlockSpec(vector.shape, lambda g, *_: (0, 0))]
            + [pl.BlockSpec(memory_space=pl.ANY)] * len(after),
            out_specs=[pl.BlockSpec(shape, lambda g, *_: (0, 0, 0))] * count,
        ),
        out_shape=[jax.ShapeDtypeStruct(shape, f32)] * count,
        compiler_params=params(),
        cost_estimate=cost(0, 0),
        name="gather_blocks",
    )(slots, vector, *after)


def beta_sum(vector, received, slots, signs, pair_index, pair_tables, after, dots=None, with_dot=False, work=0):
    rows, cols = vector.shape
    blocks = cols // SB
    npair = pair_tables.shape[0]
    kb = slots.shape[0]
    far = len(received)
    each = received[0].shape[0]
    dots = [] if dots is None else dots
    per = divisor(blocks, 16)
    steps = blocks // per

    def kernel(slots_ref, sign_ref, pair_ref, *refs):
        v_ref, t_ref = refs[:2]
        r_refs = refs[2 : 2 + far]
        at = 2 + far + len(after)
        dot_refs = refs[at : at + len(dots)]
        out_ref = refs[at + len(dots)]
        pool, wide, t_high, t_low, sems = refs[-5:]
        g = pl.program_id(0)

        @pl.when(g == 0)
        def _():
            copies = [
                pltpu.make_async_copy(r_refs[i], pool.at[pl.ds(i * each, each)], sems.at[i]) for i in range(far)
            ]
            for copy in copies:
                copy.start()
            for p in range(npair):
                high, low = halves(t_ref[p])
                t_high[p * SB : (p + 1) * SB, :] = high
                t_low[p * SB : (p + 1) * SB, :] = low
            for copy in copies:
                copy.wait()

        wide[...] = jnp.zeros_like(wide)
        for t in range(per):
            target = g * per + t
            for k in range(kb):
                slot = slots_ref[k, target]
                own = v_ref[:, pl.ds(pl.multiple_of(lax.min(slot, blocks - 1) * SB, SB), SB)]
                other = pool[lax.max(slot - blocks, 0)]
                block = jnp.where(slot < blocks, own, other) * sign_ref[k, target].astype(f32)
                at = pl.ds(pl.multiple_of(pair_ref[k, target] * SB, SB), SB)
                wide[t * rows : (t + 1) * rows, at] += block
        high, low = halves(wide[...])
        total = mul(high, t_high[...]) + mul(low, t_high[...]) + mul(high, t_low[...])
        for t in range(per):
            out_ref[:, t * SB : (t + 1) * SB] = total[t * rows : (t + 1) * rows]
        if with_dot:
            sums_ref = refs[-6]
            dot = jnp.zeros((rows, SB), f32)
            square = jnp.zeros((rows, SB), f32)
            for t in range(per):
                v = v_ref[:, pl.ds(pl.multiple_of((g * per + t) * SB, SB), SB)]
                dot = dot + total[t * rows : (t + 1) * rows] * v
                square = square + v * v
            dot = jnp.sum(dot, axis=0, keepdims=True)
            square = jnp.sum(square, axis=0, keepdims=True)

            @pl.when(g == 0)
            def _():
                sums_ref[...] = jnp.zeros_like(sums_ref)

            sums_ref[0:1, :] += dot
            if dots:
                sums_ref[1:2, :] += square

            @pl.when(g == steps - 1)
            def _():
                value = sums_ref[...]
                for ref in dot_refs:
                    for at in range(0, ref.shape[1], SB):
                        first = lax.broadcasted_iota(jnp.int32, value.shape, 0) == 0
                        value = value + jnp.where(first, ref[:, at : at + SB], 0.0)
                sums_ref[...] = value

    out = pl.pallas_call(
        kernel,
        grid_spec=pltpu.PrefetchScalarGridSpec(
            num_scalar_prefetch=3,
            grid=(steps,),
            in_specs=[
                pl.BlockSpec((rows, cols), lambda g, *_: (0, 0)),
                pl.BlockSpec(pair_tables.shape, lambda g, *_: (0, 0, 0)),
            ]
            + [pl.BlockSpec(memory_space=pl.ANY)] * (far + len(after))
            + [pl.BlockSpec(dot.shape, lambda g, *_: (0, 0)) for dot in dots],
            out_specs=[pl.BlockSpec((rows, per * SB), lambda g, *_: (0, g))]
            + ([pl.BlockSpec((8, SB), lambda g, *_: (0, 0))] if with_dot else []),
            scratch_shapes=[
                pltpu.VMEM((far * each, rows, SB), f32),
                pltpu.VMEM((per * rows, npair * SB), f32),
                pltpu.VMEM((npair * SB, SB), bf16),
                pltpu.VMEM((npair * SB, SB), bf16),
                pltpu.SemaphoreType.DMA((far,)),
            ],
        ),
        out_shape=[jax.ShapeDtypeStruct((rows, cols), f32)]
        + ([jax.ShapeDtypeStruct((8, SB), f32)] if with_dot else []),
        compiler_params=params(),
        cost_estimate=cost(work, work // 300),
        name="beta_sum",
    )(slots, signs, pair_index, vector, pair_tables, *received, *after, *dots)
    return list(out)


def correct(returned, beta_term, device, wide, narrow, extra, previous):
    rows, cols = beta_term.shape
    parts = returned.shape[0]
    sums = [] if extra is None else extra[0]
    wholes = [beta_term] + ([] if extra is None else [extra[1], extra[2]])
    count = len(wholes)
    sent = parts if previous else 1

    def kernel(device_ref, *refs):
        sum_refs = refs[: len(sums)]
        whole_refs = refs[len(sums) :][:count]
        part_ref = refs[len(sums) + count]
        out_refs = refs[len(sums) + count + 1 + len(previous) :][: 1 + sent]
        held, sems, out_sems = refs[-3:]
        pieces = []
        for j in range(parts):
            if previous:
                place = device_ref[0] ^ j
                at = pl.multiple_of(parts * wide + place * narrow, SB)
                pieces.append((held, j, at, part_ref.at[place, :, wide:], out_refs[1 + j]))
            else:
                pieces.append((held, j, j * wide, part_ref.at[j, :, :wide], out_refs[1].at[j]))
        taken = []
        given = []
        for p, (buffer, j, start, part, target) in enumerate(pieces):
            at = pl.ds(start, buffer.shape[-1])
            taken.append(
                [pltpu.make_async_copy(whole_refs[i].at[:, at], buffer.at[i, j], sems.at[i, p]) for i in range(count)]
                + [pltpu.make_async_copy(part, buffer.at[count, j], sems.at[count, p])]
            )
            given.append([pltpu.make_async_copy(buffer.at[count, j], out_refs[0].at[:, at], out_sems.at[0, p])])
            given[-1].append(pltpu.make_async_copy(buffer.at[count, j], target, out_sems.at[1, p]))
        for copies in taken:
            for copy in copies:
                copy.start()
        if extra is not None:
            total = sum_refs[0][...]
            for ref in sum_refs[1:]:
                total = total + ref[...]
            both = [jnp.sum(total[i : i + 1], axis=1, keepdims=True) for i in range(2)]
            theta = both[0] / both[1]
        for p, (buffer, j, _, _, _) in enumerate(pieces):
            for copy in taken[p]:
                copy.wait()
            value = buffer[0, j] + buffer[count, j]
            if extra is not None:
                value = (value - theta * buffer[1, j]) / buffer[2, j]
            buffer[count, j] = value
            for copy in given[p]:
                copy.start()
        for copies in given:
            for copy in copies:
                copy.wait()

    anywhere = pl.BlockSpec(memory_space=pl.ANY)
    shapes = [(rows, cols)] + ([(rows, narrow)] * parts if previous else [(parts, rows, wide)])
    out = pl.pallas_call(
        kernel,
        in_specs=[pl.BlockSpec(memory_space=pltpu.SMEM)]
        + [pl.BlockSpec(memory_space=pltpu.VMEM)] * len(sums)
        + [anywhere] * (count + 1 + len(previous)),
        out_specs=[anywhere] * (1 + sent),
        out_shape=[jax.ShapeDtypeStruct(shape, f32) for shape in shapes],
        input_output_aliases={1 + len(sums) + count + 1: 0} if previous else {},
        scratch_shapes=[
            pltpu.VMEM((count + 1, parts, rows, narrow if previous else wide), f32),
            pltpu.SemaphoreType.DMA((count + 1, parts)),
            pltpu.SemaphoreType.DMA((2, parts)),
        ],
        compiler_params=params(),
        cost_estimate=cost(0, 0),
        name="correct",
    )(device, *sums, *wholes, returned, *previous)
    return out[0], out[1:]


def finish(returned, beta_term, device, start, previous, extra=None, work=0):
    rows, cols = beta_term.shape
    listed = isinstance(returned, (list, tuple))
    arrays = list(returned) if listed else [returned]
    parts = len(arrays) if listed else returned.shape[0]
    width = arrays[0].shape[-1]
    sums = [] if extra is None else extra[0]
    wholes = [beta_term] + ([] if extra is None else [extra[1], extra[2]])
    count = len(wholes)
    aliased = [] if previous is None else [previous]
    sent = [] if extra is None else arrays

    def kernel(device_ref, *refs):
        sum_refs = refs[: len(sums)]
        whole_refs = refs[len(sums) :][:count]
        part_refs = refs[len(sums) + count :][: len(arrays)]
        out_refs = refs[len(sums) + count + len(arrays) + len(aliased) :][: 1 + len(sent)]
        held, sems, out_sems = refs[-3:]

        def piece(among, j):
            return among[j] if listed else among[0].at[j]

        taken = []
        given = []
        for j in range(parts):
            place = device_ref[0] ^ j if listed else j
            at = pl.ds(pl.multiple_of(start + place * width, SB), width)
            taken.append(
                [pltpu.make_async_copy(whole_refs[i].at[:, at], held.at[i, j], sems.at[i, j]) for i in range(count)]
                + [pltpu.make_async_copy(piece(part_refs, j), held.at[count, j], sems.at[count, j])]
            )
            given.append([pltpu.make_async_copy(held.at[count, j], out_refs[0].at[:, at], out_sems.at[0, j])])
            if sent:
                target = piece(out_refs[1:], j)
                given[-1].append(pltpu.make_async_copy(held.at[count, j], target, out_sems.at[1, j]))
        for copies in taken:
            for copy in copies:
                copy.start()
        if extra is not None:
            total = sum_refs[0][...]
            for ref in sum_refs[1:]:
                total = total + ref[...]
            both = [jnp.sum(total[i : i + 1], axis=1, keepdims=True) for i in range(2)]
            theta = both[0] / both[1]
        for j in range(parts):
            for copy in taken[j]:
                copy.wait()
            value = held[0, j] + held[count, j]
            if extra is not None:
                value = (value - theta * held[1, j]) / held[2, j]
            held[count, j] = value
            for copy in given[j]:
                copy.start()
        for copies in given:
            for copy in copies:
                copy.wait()

    anywhere = pl.BlockSpec(memory_space=pl.ANY)
    out = pl.pallas_call(
        kernel,
        in_specs=[pl.BlockSpec(memory_space=pltpu.SMEM)]
        + [pl.BlockSpec(memory_space=pltpu.VMEM)] * len(sums)
        + [anywhere] * (count + len(arrays) + len(aliased)),
        out_specs=[anywhere] * (1 + len(sent)),
        out_shape=[jax.ShapeDtypeStruct(a.shape, f32) for a in [beta_term] + sent],
        input_output_aliases={1 + len(sums) + count + len(arrays): 0} if aliased else {},
        scratch_shapes=[
            pltpu.VMEM((count + 1, parts, rows, width), f32),
            pltpu.SemaphoreType.DMA((count + 1, parts)),
            pltpu.SemaphoreType.DMA((2, parts)),
        ],
        compiler_params=params(),
        cost_estimate=cost(work, work // 300),
        name="finish" if extra is None else "correct",
    )(device, *sums, *wholes, *arrays, *aliased)
    return out[0], out[1:]


def make_local(n_alpha, n_beta):
    chips = n_alpha // 2

    def to_partners(parts):
        return [lax.ppermute(part, "beta", [(i, i ^ k) for i in range(n_beta)]) for k, part in enumerate(parts, 1)]

    def turn(parts):
        return lax.all_to_all(parts, "alpha", 0, 0, tiled=True)

    def swap(parts):
        moved = list(parts)
        for k in range(n_alpha - 1, 0, -1):
            moved[k] = lax.ppermute(parts[k], "alpha", [(i, i ^ k) for i in range(n_alpha)])
        return moved

    def local(
        start_vector,
        precondition,
        alpha_hamiltonian,
        alpha_pairs,
        pair_tables,
        source_blocks,
        pair_index,
        phase_signs,
        cross_pairs,
        cross_signs,
    ):
        rows, cols = start_vector.shape
        blocks = cols // SB
        mine = blocks // n_alpha
        few = max(1, round(mine * SHARE))
        wide, narrow = (mine - few) * SB, few * SB
        border = n_alpha * wide
        cap = (blocks + 1) // 2
        device = lax.axis_index("alpha").astype(jnp.int32).reshape(1)
        me = lax.axis_index("beta").astype(jnp.int32)

        sent, sent_few = pack(start_vector, device, n_alpha, wide, narrow)
        arrived = turn(sent)
        arrived_few = swap(sent_few)

        *marks, found = mark(source_blocks, me.reshape(1), n_beta, [sent])
        worst = marks[0][1:2, :1]
        marks = to_partners(marks)
        for other in marks:
            worst = jnp.maximum(worst, other[1:2, :1])
        too_many = worst[0, 0] > cap
        pairs_by_k = pair_index.T

        def plan(r):
            partner = (source_blocks // blocks) ^ me
            here = (found >= r * cap) & (found < (r + 1) * cap) & (partner != 0)
            far_slot = blocks + (partner - 1) * (cap + 1) + found - r * cap
            mine = (partner == 0) & (r == 0)
            slots = jnp.where(mine, source_blocks - me * blocks, jnp.where(here, far_slot, 0))
            signs = jnp.where(mine | here, phase_signs, 0)
            return positions(marks, r * cap, cap), slots.T, signs.T

        first_plan = plan(0)

        def beta_send(vector, planned, after):
            sent = gather_blocks(vector, planned[0], n_beta - 1, cap, after)
            received = to_partners(sent)
            return received, (received[:2], received[2:])

        def beta_round(vector, received, planned, after, dots=None, with_dot=False, work=0):
            _, slots, signs = planned
            return beta_sum(vector, received, slots, signs, pairs_by_k, pair_tables, after, dots, with_dot, work)

        def beta_side(vector, received, after, dots=None, with_dot=False, work=0):
            done = beta_round(vector, received, first_plan, after, dots, with_dot, work)

            def more(done):
                for r in range(1, -(-blocks // cap)):
                    planned = plan(r)
                    added = beta_round(vector, beta_send(vector, planned, [])[0], planned, [], None, with_dot)
                    done = [a + b for a, b in zip(done, added)]
                return done

            return lax.cond(too_many, more, lambda done: done, done)

        received, token = beta_send(start_vector, first_plan, [])
        prepared = prepare(alpha_hamiltonian, alpha_pairs, pair_tables, [])
        common = (prepared, cross_pairs, cross_signs, device)
        width = wide + narrow
        columns = arrived.reshape(n_alpha * rows, wide)
        first = alpha_sum([columns], *common, 0, token[0], WORK, width, 0, [])
        (total,) = alpha_sum(arrived_few, *common, border // SB, [], 0, width, wide, first)
        returned = turn(total.reshape(n_alpha, rows, width))
        dots = [jnp.sum(columns * total[:, :wide], axis=0, keepdims=True)]
        last = total[:, wide:].reshape(n_alpha, rows, narrow)
        few = [lax.dynamic_index_in_dim(last, device[0] ^ k, 0, keepdims=False) for k in range(n_alpha)]
        dots.append(sum(jnp.sum(a * b, axis=0, keepdims=True) for a, b in zip(arrived_few, few)))
        beta_term, sums = beta_side(start_vector, received, [], dots, True)
        for other in to_partners([sums] * (n_beta - 1)):
            sums = sums + other
        sums = sums + lax.ppermute(sums, "alpha", [(i, i ^ 1) for i in range(n_alpha)])
        all_sums = [sums]
        for k in range(1, chips):
            pairs = [(i, ((i // 2 + k) % chips) * 2 + i % 2) for i in range(n_alpha)]
            all_sums.append(lax.ppermute(sums, "alpha", pairs))

        extra = (all_sums, start_vector, precondition)
        correction, (parts,) = correct(returned, beta_term, device, wide, narrow, extra, [])
        arrived = turn(parts)
        correction, few = correct(returned, beta_term, device, wide, narrow, extra, [correction])
        arrived_few = swap(few)
        received, token = beta_send(correction, first_plan, [])
        columns = arrived.reshape(n_alpha * rows, wide)
        (total,) = alpha_sum([columns], *common, 0, token[0], WORK, wide, 0, [])
        returned = turn(total.reshape(n_alpha, rows, wide))
        totals = alpha_sum(arrived_few, *common, border // SB, [total, *token[1]], 10 * WORK, 0, 0, [])
        returned_few = swap(totals)
        (beta_term,) = beta_side(correction, received, totals[:1], work=WORK)
        sigma_next, _ = finish(returned, beta_term, device, 0, None, None, WORK)
        sigma_next, _ = finish(returned_few, beta_term, device, border, sigma_next)
        return correction, sigma_next

    return local


def solution(mesh):
    placed = (
        P("alpha", "beta"),
        P("alpha", "beta"),
        P(),
        P(),
        P(),
        P("beta", None),
        P("beta", None),
        P("beta", None),
        P(None, "beta"),
        P(None, "beta"),
    )
    return jax.shard_map(
        make_local(mesh.shape["alpha"], mesh.shape["beta"]),
        mesh=mesh,
        in_specs=placed,
        out_specs=(P("alpha", "beta"), P("alpha", "beta")),
        check_vma=False,
    )
```

```python
import jax
import jax.numpy as jnp
from jax import lax
from jax.experimental import pallas as pl
from jax.experimental.pallas import tpu as pltpu
from jax.sharding import PartitionSpec as P

SB = 128
SHARE = 0.375
WORK = 20_000_000_000
VMEM_BYTES = 60 * 1024 * 1024
f32 = jnp.float32
bf16 = jnp.bfloat16


def params():
    return pltpu.CompilerParams(vmem_limit_bytes=VMEM_BYTES)


def divisor(number, most):
    return max(d for d in range(1, most + 1) if number % d == 0)


def halves(x):
    high = x.astype(bf16)
    return high, (x - high.astype(f32)).astype(bf16)


def mul(a, b):
    return jnp.dot(a, b, preferred_element_type=f32)


def cost(flops, count):
    return pl.CostEstimate(flops=max(flops, 1), bytes_accessed=max(count, 1), transcendentals=0)


def prepare(alpha_hamiltonian, alpha_pairs, pair_tables, after):
    size = alpha_hamiltonian.shape[0]
    nq = alpha_pairs.shape[0]
    depth = (nq + 1) * size
    npair = pair_tables.shape[0]

    def kernel(h_ref, p_ref, t_ref, *refs):
        a_twice, a_low, t_high, t_low = refs[-4:]
        for q in range(nq + 1):
            high, low = halves(h_ref[...] if q == 0 else p_ref[q - 1])
            a_twice[:, q * size : (q + 1) * size] = high
            a_twice[:, depth + q * size : depth + (q + 1) * size] = high
            a_low[:, q * size : (q + 1) * size] = low
        for p in range(npair):
            high, low = halves(t_ref[p])
            t_high[p, :SB, :] = high
            t_high[p, SB:, :] = high
            t_low[p] = low

    shapes = [(size, 2 * depth), (size, depth), (npair, 2 * SB, SB), (npair, SB, SB)]
    return pl.pallas_call(
        kernel,
        in_specs=[pl.BlockSpec(memory_space=pltpu.VMEM)] * 3 + [pl.BlockSpec(memory_space=pl.ANY)] * len(after),
        out_specs=[pl.BlockSpec(memory_space=pltpu.VMEM)] * 4,
        out_shape=[jax.ShapeDtypeStruct(shape, bf16) for shape in shapes],
        compiler_params=params(),
        cost_estimate=cost(0, 0),
        name="prepare",
    )(alpha_hamiltonian, alpha_pairs, pair_tables, *after)


def pack(vector, device, parts, start, width, listed, after):
    rows = vector.shape[0]

    def kernel(device_ref, source, *refs):
        targets = refs[len(after) : -2]
        held, sems = refs[-2:]
        taken = []
        given = []
        for j in range(parts):
            at = pl.multiple_of(start + ((device_ref[0] ^ j) if listed else j) * width, SB)
            target = targets[j] if listed else targets[0].at[j]
            taken.append(pltpu.make_async_copy(source.at[:, pl.ds(at, width)], held.at[j], sems.at[0, j]))
            given.append(pltpu.make_async_copy(held.at[j], target, sems.at[1, j]))
        for copy in taken:
            copy.start()
        for first, second in zip(taken, given):
            first.wait()
            second.start()
        for copy in given:
            copy.wait()

    anywhere = pl.BlockSpec(memory_space=pl.ANY)
    shapes = [(rows, width)] * parts if listed else [(parts, rows, width)]
    return pl.pallas_call(
        kernel,
        in_specs=[pl.BlockSpec(memory_space=pltpu.SMEM)] + [anywhere] * (1 + len(after)),
        out_specs=[anywhere] * len(shapes),
        out_shape=[jax.ShapeDtypeStruct(shape, f32) for shape in shapes],
        scratch_shapes=[pltpu.VMEM((parts, rows, width), f32), pltpu.SemaphoreType.DMA((2, parts))],
        compiler_params=params(),
        cost_estimate=cost(0, 0),
        name="pack",
    )(device, vector, *after)


def alpha_sum(columns, prepared, cross_pairs, cross_signs, device, start, after, work, full, offset, previous):
    size, width = prepared[1].shape[0], columns[0].shape[1]
    count = len(columns)
    rows = size // count
    depth = prepared[1].shape[1]
    nq = cross_pairs.shape[0]
    blocks = width // SB
    per = divisor(blocks, 9)
    steps = blocks // per
    wide = per * SB

    def kernel(device_ref, pairs_ref, signs_ref, *refs):
        v_any = refs[:count]
        prepared_any = refs[count : count + 4]
        outs = refs[count + 4 + len(after) + len(previous) :][: 1 if full else count]
        v_held, out_held, a_twice, a_low, t_high, t_low, even, odd, sems, once = refs[-10:]

        def at(g):
            return pl.ds(pl.multiple_of(g * wide, SB), wide)

        def row(k):
            return pl.ds(pl.multiple_of((device_ref[0] ^ k) * rows, rows) if count > 1 else 0, rows)

        class Several:
            def __init__(self, copies):
                self.copies = copies

            def start(self):
                for copy in self.copies:
                    copy.start()

            def wait(self):
                for copy in self.copies:
                    copy.wait()

        def taken(g):
            return Several(
                [
                    pltpu.make_async_copy(v_any[k].at[:, at(g)], v_held.at[g, row(k)], sems.at[0, g, k])
                    for k in range(count)
                ]
            )

        def given(g):
            if full:
                to = pl.ds(offset + g * wide, wide)
                return pltpu.make_async_copy(out_held.at[g], outs[0].at[:, to], sems.at[1, g, 0])
            return Several(
                [
                    pltpu.make_async_copy(out_held.at[g, row(k)], outs[k].at[:, at(g)], sems.at[1, g, k])
                    for k in range(count)
                ]
            )

        held = (a_twice, a_low, t_high, t_low)
        loads = [pltpu.make_async_copy(prepared_any[i], held[i], once.at[i]) for i in range(4)]
        for load in loads[2:]:
            load.start()
        taken(0).start()
        for load in loads[:2]:
            load.start()
        for g in range(1, steps):
            taken(g).start()
        for load in loads[2:]:
            load.wait()

        def build(g, b):
            high, low = halves(v_held[g])
            b[:size, :] = high
            b[depth : depth + size, :] = low
            first = start + device_ref[0] * blocks + g * per
            for t in range(per):
                here = slice(t * SB, (t + 1) * SB)
                both = jnp.concatenate([high[:, here], low[:, here]], axis=1)
                chosen = [pairs_ref[q, first + t] for q in range(nq)]
                x = mul(both, jnp.concatenate([t_high[p] for p in chosen], axis=1))
                x = x + mul(high[:, here], jnp.concatenate([t_low[p] for p in chosen], axis=1))
                for q in range(nq):
                    x_high, x_low = halves(x[:, q * SB : (q + 1) * SB] * signs_ref[q, first + t].astype(f32))
                    row = (q + 1) * size
                    b[row : row + size, here] = x_high
                    b[depth + row : depth + row + size, here] = x_low

        taken(0).wait()
        build(0, even)
        for load in loads[:2]:
            load.wait()
        for g in range(steps):
            b, other = (even, odd) if g % 2 == 0 else (odd, even)
            if g + 1 < steps:
                taken(g + 1).wait()
                build(g + 1, other)
            out_held[g] = mul(a_twice[...], b[...]) + mul(a_low[...], b[:depth, :])
            given(g).start()
        for g in range(steps):
            given(g).wait()

    anywhere = pl.BlockSpec(memory_space=pl.ANY)
    return pl.pallas_call(
        kernel,
        in_specs=[pl.BlockSpec(memory_space=pltpu.SMEM)] * 3 + [anywhere] * (count + 4 + len(after) + len(previous)),
        out_specs=[anywhere] * (1 if full else count),
        out_shape=[jax.ShapeDtypeStruct((size, full), f32)]
        if full
        else [jax.ShapeDtypeStruct((rows, width), f32)] * count,
        input_output_aliases={3 + count + 4 + len(after): 0} if previous else {},
        scratch_shapes=[pltpu.VMEM((steps, size, wide), f32)] * 2
        + [pltpu.VMEM(a.shape, bf16) for a in prepared]
        + [
            pltpu.VMEM((2 * depth, wide), bf16),
            pltpu.VMEM((2 * depth, wide), bf16),
            pltpu.SemaphoreType.DMA((2, steps, count)),
            pltpu.SemaphoreType.DMA((4,)),
        ],
        compiler_params=params(),
        cost_estimate=cost(work, work // 300),
        name="alpha_sum",
    )(device, cross_pairs, cross_signs, *columns, *prepared, *after, *previous)


def earlier(lanes):
    row = lax.broadcasted_iota(jnp.int32, (lanes, lanes), 0)
    column = lax.broadcasted_iota(jnp.int32, (lanes, lanes), 1)
    return jnp.where(row < column, 1.0, 0.0).astype(bf16)


def mark(source_blocks, me, parts, after):
    blocks, kb = source_blocks.shape
    lanes = -(-blocks // SB) * SB
    tall = -(-parts // 8) * 8

    def kernel(me_ref, source_ref, *refs):
        marks_refs = refs[len(after) : len(after) + parts - 1]
        found_ref, held = refs[-2:]
        lane = lax.broadcasted_iota(jnp.int32, (blocks, lanes), 1)

        def hit(s, k):
            return (source_ref[:, k : k + 1] - s * blocks == lane) & (lane < blocks)

        held[...] = jnp.zeros_like(held)
        worst = jnp.zeros((1, 1), f32)
        for s in range(parts):
            needed = jnp.zeros((1, lanes), f32)
            for k in range(kb):
                needed = jnp.maximum(needed, jnp.max(jnp.where(hit(s, k), 1.0, 0.0), axis=0, keepdims=True))
            held[s : s + 1, :] = needed
            count = jnp.sum(needed, axis=1, keepdims=True)
            worst = jnp.maximum(worst, jnp.where(me_ref[0] == s, 0.0, count))
        place = mul(held[...].astype(bf16), earlier(lanes))
        for k in range(kb):
            found = jnp.zeros((blocks, 1), f32)
            for s in range(parts):
                found = found + jnp.sum(jnp.where(hit(s, k), place[s : s + 1, :], 0.0), axis=1, keepdims=True)
            found_ref[:, k : k + 1] = found.astype(jnp.int32)
        for k, marks_ref in enumerate(marks_refs, 1):
            marks_ref[...] = jnp.zeros_like(marks_ref)
            marks_ref[0:1, :] = held[pl.ds(me_ref[0] ^ k, 1), :]
            marks_ref[1:2, :] = jnp.broadcast_to(worst, (1, lanes))

    return pl.pallas_call(
        kernel,
        in_specs=[pl.BlockSpec(memory_space=pltpu.SMEM), pl.BlockSpec(memory_space=pltpu.VMEM)]
        + [pl.BlockSpec(memory_space=pl.ANY)] * len(after),
        out_specs=[pl.BlockSpec(memory_space=pltpu.VMEM)] * parts,
        out_shape=[jax.ShapeDtypeStruct((8, lanes), f32)] * (parts - 1)
        + [jax.ShapeDtypeStruct((blocks, kb), jnp.int32)],
        scratch_shapes=[pltpu.VMEM((tall, lanes), f32)],
        compiler_params=params(),
        cost_estimate=cost(0, 0),
        name="mark",
    )(me, source_blocks, *after)


def positions(marks, first, cap):
    lanes = marks[0].shape[1]
    count = len(marks)
    tall = -(-count // 8) * 8

    def kernel(*refs):
        out_ref, held = refs[-2:]
        held[...] = jnp.zeros_like(held)
        for k in range(count):
            held[k : k + 1, :] = refs[k][0:1, :]
        needed = held[...]
        slot = mul(needed.astype(bf16), earlier(lanes)).astype(jnp.int32) - first
        out_ref[...] = jnp.where((needed > 0) & (slot >= 0) & (slot < cap), slot, cap)

    return pl.pallas_call(
        kernel,
        in_specs=[pl.BlockSpec(memory_space=pltpu.VMEM)] * count,
        out_specs=pl.BlockSpec(memory_space=pltpu.VMEM),
        out_shape=jax.ShapeDtypeStruct((tall, lanes), jnp.int32),
        scratch_shapes=[pltpu.VMEM((tall, lanes), f32)],
        compiler_params=params(),
        cost_estimate=cost(0, 0),
        name="positions",
    )(*marks)


def gather_blocks(vector, slots, count, cap, after):
    rows, cols = vector.shape

    def kernel(slots_ref, v_ref, *refs):
        outs = refs[len(after) :]

        @pl.loop(0, cols // SB, unroll=4)
        def _(b):
            block = v_ref[:, pl.ds(pl.multiple_of(b * SB, SB), SB)]
            for k in range(count):
                outs[k][slots_ref[k, b]] = block

    shape = (cap + 1, rows, SB)
    return pl.pallas_call(
        kernel,
        grid_spec=pltpu.PrefetchScalarGridSpec(
            num_scalar_prefetch=1,
            grid=(1,),
            in_specs=[pl.BlockSpec(vector.shape, lambda g, *_: (0, 0))]
            + [pl.BlockSpec(memory_space=pl.ANY)] * len(after),
            out_specs=[pl.BlockSpec(shape, lambda g, *_: (0, 0, 0))] * count,
        ),
        out_shape=[jax.ShapeDtypeStruct(shape, f32)] * count,
        compiler_params=params(),
        cost_estimate=cost(0, 0),
        name="gather_blocks",
    )(slots, vector, *after)


def beta_sum(vector, received, slots, signs, pair_index, pair_tables, after, dots=None, with_dot=False, work=0):
    rows, cols = vector.shape
    blocks = cols // SB
    npair = pair_tables.shape[0]
    kb = slots.shape[0]
    far = len(received)
    each = received[0].shape[0]
    dots = [] if dots is None else dots
    per = divisor(blocks, 16)
    steps = blocks // per

    def kernel(slots_ref, sign_ref, pair_ref, *refs):
        v_ref, t_ref = refs[:2]
        r_refs = refs[2 : 2 + far]
        at = 2 + far + len(after)
        dot_refs = refs[at : at + len(dots)]
        out_ref = refs[at + len(dots)]
        pool, wide, t_high, t_low, sems = refs[-5:]
        g = pl.program_id(0)

        @pl.when(g == 0)
        def _():
            copies = [
                pltpu.make_async_copy(r_refs[i], pool.at[pl.ds(i * each, each)], sems.at[i]) for i in range(far)
            ]
            for copy in copies:
                copy.start()
            for p in range(npair):
                high, low = halves(t_ref[p])
                t_high[p * SB : (p + 1) * SB, :] = high
                t_low[p * SB : (p + 1) * SB, :] = low
            for copy in copies:
                copy.wait()

        wide[...] = jnp.zeros_like(wide)
        for t in range(per):
            target = g * per + t
            for k in range(kb):
                slot = slots_ref[k, target]
                own = v_ref[:, pl.ds(pl.multiple_of(lax.min(slot, blocks - 1) * SB, SB), SB)]
                other = pool[lax.max(slot - blocks, 0)]
                block = jnp.where(slot < blocks, own, other) * sign_ref[k, target].astype(f32)
                at = pl.ds(pl.multiple_of(pair_ref[k, target] * SB, SB), SB)
                wide[t * rows : (t + 1) * rows, at] += block
        high, low = halves(wide[...])
        total = mul(high, t_high[...]) + mul(low, t_high[...]) + mul(high, t_low[...])
        for t in range(per):
            out_ref[:, t * SB : (t + 1) * SB] = total[t * rows : (t + 1) * rows]
        if with_dot:
            sums_ref = refs[-6]
            dot = jnp.zeros((rows, SB), f32)
            square = jnp.zeros((rows, SB), f32)
            for t in range(per):
                v = v_ref[:, pl.ds(pl.multiple_of((g * per + t) * SB, SB), SB)]
                dot = dot + total[t * rows : (t + 1) * rows] * v
                square = square + v * v
            dot = jnp.sum(dot, axis=0, keepdims=True)
            square = jnp.sum(square, axis=0, keepdims=True)

            @pl.when(g == 0)
            def _():
                sums_ref[...] = jnp.zeros_like(sums_ref)

            sums_ref[0:1, :] += dot
            if dots:
                sums_ref[1:2, :] += square

            @pl.when(g == steps - 1)
            def _():
                value = sums_ref[...]
                for ref in dot_refs:
                    for at in range(0, ref.shape[1], SB):
                        first = lax.broadcasted_iota(jnp.int32, value.shape, 0) == 0
                        value = value + jnp.where(first, ref[:, at : at + SB], 0.0)
                sums_ref[...] = value

    out = pl.pallas_call(
        kernel,
        grid_spec=pltpu.PrefetchScalarGridSpec(
            num_scalar_prefetch=3,
            grid=(steps,),
            in_specs=[
                pl.BlockSpec((rows, cols), lambda g, *_: (0, 0)),
                pl.BlockSpec(pair_tables.shape, lambda g, *_: (0, 0, 0)),
            ]
            + [pl.BlockSpec(memory_space=pl.ANY)] * (far + len(after))
            + [pl.BlockSpec(dot.shape, lambda g, *_: (0, 0)) for dot in dots],
            out_specs=[pl.BlockSpec((rows, per * SB), lambda g, *_: (0, g))]
            + ([pl.BlockSpec((8, SB), lambda g, *_: (0, 0))] if with_dot else []),
            scratch_shapes=[
                pltpu.VMEM((far * each, rows, SB), f32),
                pltpu.VMEM((per * rows, npair * SB), f32),
                pltpu.VMEM((npair * SB, SB), bf16),
                pltpu.VMEM((npair * SB, SB), bf16),
                pltpu.SemaphoreType.DMA((far,)),
            ],
        ),
        out_shape=[jax.ShapeDtypeStruct((rows, cols), f32)]
        + ([jax.ShapeDtypeStruct((8, SB), f32)] if with_dot else []),
        compiler_params=params(),
        cost_estimate=cost(work, work // 300),
        name="beta_sum",
    )(slots, signs, pair_index, vector, pair_tables, *received, *after, *dots)
    return list(out)


def correct(returned, beta_term, device, wide, narrow, extra, previous):
    rows, cols = beta_term.shape
    parts = returned.shape[0]
    sums = [] if extra is None else extra[0]
    wholes = [beta_term] + ([] if extra is None else [extra[1], extra[2]])
    count = len(wholes)
    sent = parts if previous else 1

    def kernel(device_ref, *refs):
        sum_refs = refs[: len(sums)]
        whole_refs = refs[len(sums) :][:count]
        part_ref = refs[len(sums) + count]
        out_refs = refs[len(sums) + count + 1 + len(previous) :][: 1 + sent]
        held, sems, out_sems = refs[-3:]
        pieces = []
        for j in range(parts):
            if previous:
                place = device_ref[0] ^ j
                at = pl.multiple_of(parts * wide + place * narrow, SB)
                pieces.append((held, j, at, part_ref.at[place, :, wide:], out_refs[1 + j]))
            else:
                pieces.append((held, j, j * wide, part_ref.at[j, :, :wide], out_refs[1].at[j]))
        taken = []
        given = []
        for p, (buffer, j, start, part, target) in enumerate(pieces):
            at = pl.ds(start, buffer.shape[-1])
            taken.append(
                [pltpu.make_async_copy(whole_refs[i].at[:, at], buffer.at[i, j], sems.at[i, p]) for i in range(count)]
                + [pltpu.make_async_copy(part, buffer.at[count, j], sems.at[count, p])]
            )
            given.append([pltpu.make_async_copy(buffer.at[count, j], out_refs[0].at[:, at], out_sems.at[0, p])])
            given[-1].append(pltpu.make_async_copy(buffer.at[count, j], target, out_sems.at[1, p]))
        for copies in taken:
            for copy in copies:
                copy.start()
        if extra is not None:
            total = sum_refs[0][...]
            for ref in sum_refs[1:]:
                total = total + ref[...]
            both = [jnp.sum(total[i : i + 1], axis=1, keepdims=True) for i in range(2)]
            theta = both[0] / both[1]
        for p, (buffer, j, _, _, _) in enumerate(pieces):
            for copy in taken[p]:
                copy.wait()
            value = buffer[0, j] + buffer[count, j]
            if extra is not None:
                value = (value - theta * buffer[1, j]) / buffer[2, j]
            buffer[count, j] = value
            for copy in given[p]:
                copy.start()
        for copies in given:
            for copy in copies:
                copy.wait()

    anywhere = pl.BlockSpec(memory_space=pl.ANY)
    shapes = [(rows, cols)] + ([(rows, narrow)] * parts if previous else [(parts, rows, wide)])
    out = pl.pallas_call(
        kernel,
        in_specs=[pl.BlockSpec(memory_space=pltpu.SMEM)]
        + [pl.BlockSpec(memory_space=pltpu.VMEM)] * len(sums)
        + [anywhere] * (count + 1 + len(previous)),
        out_specs=[anywhere] * (1 + sent),
        out_shape=[jax.ShapeDtypeStruct(shape, f32) for shape in shapes],
        input_output_aliases={1 + len(sums) + count + 1: 0} if previous else {},
        scratch_shapes=[
            pltpu.VMEM((count + 1, parts, rows, narrow if previous else wide), f32),
            pltpu.SemaphoreType.DMA((count + 1, parts)),
            pltpu.SemaphoreType.DMA((2, parts)),
        ],
        compiler_params=params(),
        cost_estimate=cost(0, 0),
        name="correct",
    )(device, *sums, *wholes, returned, *previous)
    return out[0], out[1:]


def finish(returned, beta_term, device, start, previous, extra=None, work=0):
    rows, cols = beta_term.shape
    listed = isinstance(returned, (list, tuple))
    arrays = list(returned) if listed else [returned]
    parts = len(arrays) if listed else returned.shape[0]
    width = arrays[0].shape[-1]
    sums = [] if extra is None else extra[0]
    wholes = [beta_term] + ([] if extra is None else [extra[1], extra[2]])
    count = len(wholes)
    aliased = [] if previous is None else [previous]
    sent = [] if extra is None else arrays

    def kernel(device_ref, *refs):
        sum_refs = refs[: len(sums)]
        whole_refs = refs[len(sums) :][:count]
        part_refs = refs[len(sums) + count :][: len(arrays)]
        out_refs = refs[len(sums) + count + len(arrays) + len(aliased) :][: 1 + len(sent)]
        held, sems, out_sems = refs[-3:]

        def piece(among, j):
            return among[j] if listed else among[0].at[j]

        taken = []
        given = []
        for j in range(parts):
            place = device_ref[0] ^ j if listed else j
            at = pl.ds(pl.multiple_of(start + place * width, SB), width)
            taken.append(
                [pltpu.make_async_copy(whole_refs[i].at[:, at], held.at[i, j], sems.at[i, j]) for i in range(count)]
                + [pltpu.make_async_copy(piece(part_refs, j), held.at[count, j], sems.at[count, j])]
            )
            given.append([pltpu.make_async_copy(held.at[count, j], out_refs[0].at[:, at], out_sems.at[0, j])])
            if sent:
                target = piece(out_refs[1:], j)
                given[-1].append(pltpu.make_async_copy(held.at[count, j], target, out_sems.at[1, j]))
        for copies in taken:
            for copy in copies:
                copy.start()
        if extra is not None:
            total = sum_refs[0][...]
            for ref in sum_refs[1:]:
                total = total + ref[...]
            both = [jnp.sum(total[i : i + 1], axis=1, keepdims=True) for i in range(2)]
            theta = both[0] / both[1]
        for j in range(parts):
            for copy in taken[j]:
                copy.wait()
            value = held[0, j] + held[count, j]
            if extra is not None:
                value = (value - theta * held[1, j]) / held[2, j]
            held[count, j] = value
            for copy in given[j]:
                copy.start()
        for copies in given:
            for copy in copies:
                copy.wait()

    anywhere = pl.BlockSpec(memory_space=pl.ANY)
    out = pl.pallas_call(
        kernel,
        in_specs=[pl.BlockSpec(memory_space=pltpu.SMEM)]
        + [pl.BlockSpec(memory_space=pltpu.VMEM)] * len(sums)
        + [anywhere] * (count + len(arrays) + len(aliased)),
        out_specs=[anywhere] * (1 + len(sent)),
        out_shape=[jax.ShapeDtypeStruct(a.shape, f32) for a in [beta_term] + sent],
        input_output_aliases={1 + len(sums) + count + len(arrays): 0} if aliased else {},
        scratch_shapes=[
            pltpu.VMEM((count + 1, parts, rows, width), f32),
            pltpu.SemaphoreType.DMA((count + 1, parts)),
            pltpu.SemaphoreType.DMA((2, parts)),
        ],
        compiler_params=params(),
        cost_estimate=cost(work, work // 300),
        name="finish" if extra is None else "correct",
    )(device, *sums, *wholes, *arrays, *aliased)
    return out[0], out[1:]


def make_local(n_alpha, n_beta):
    chips = n_alpha // 2

    def to_partners(parts):
        return [lax.ppermute(part, "beta", [(i, i ^ k) for i in range(n_beta)]) for k, part in enumerate(parts, 1)]

    def turn(parts):
        return lax.all_to_all(parts, "alpha", 0, 0, tiled=True)

    def swap(parts):
        moved = list(parts)
        for k in range(n_alpha - 1, 0, -1):
            moved[k] = lax.ppermute(parts[k], "alpha", [(i, i ^ k) for i in range(n_alpha)])
        return moved

    def local(
        start_vector,
        precondition,
        alpha_hamiltonian,
        alpha_pairs,
        pair_tables,
        source_blocks,
        pair_index,
        phase_signs,
        cross_pairs,
        cross_signs,
    ):
        rows, cols = start_vector.shape
        blocks = cols // SB
        mine = blocks // n_alpha
        few = max(1, round(mine * SHARE))
        wide, narrow = (mine - few) * SB, few * SB
        border = n_alpha * wide
        cap = (blocks + 1) // 2
        device = lax.axis_index("alpha").astype(jnp.int32).reshape(1)
        me = lax.axis_index("beta").astype(jnp.int32)

        (sent,) = pack(start_vector, device, n_alpha, 0, wide, False, [])
        arrived = turn(sent)
        sent_few = pack(start_vector, device, n_alpha, border, narrow, True, [sent])
        arrived_few = swap(sent_few)

        *marks, found = mark(source_blocks, me.reshape(1), n_beta, [sent])
        worst = marks[0][1:2, :1]
        marks = to_partners(marks)
        for other in marks:
            worst = jnp.maximum(worst, other[1:2, :1])
        too_many = worst[0, 0] > cap
        pairs_by_k = pair_index.T

        def plan(r):
            partner = (source_blocks // blocks) ^ me
            here = (found >= r * cap) & (found < (r + 1) * cap) & (partner != 0)
            far_slot = blocks + (partner - 1) * (cap + 1) + found - r * cap
            mine = (partner == 0) & (r == 0)
            slots = jnp.where(mine, source_blocks - me * blocks, jnp.where(here, far_slot, 0))
            signs = jnp.where(mine | here, phase_signs, 0)
            return positions(marks, r * cap, cap), slots.T, signs.T

        first_plan = plan(0)

        def beta_send(vector, planned, after):
            sent = gather_blocks(vector, planned[0], n_beta - 1, cap, after)
            received = to_partners(sent)
            return received, (received[:2], received[2:])

        def beta_round(vector, received, planned, after, dots=None, with_dot=False, work=0):
            _, slots, signs = planned
            return beta_sum(vector, received, slots, signs, pairs_by_k, pair_tables, after, dots, with_dot, work)

        def beta_side(vector, received, after, dots=None, with_dot=False, work=0):
            done = beta_round(vector, received, first_plan, after, dots, with_dot, work)

            def more(done):
                for r in range(1, -(-blocks // cap)):
                    planned = plan(r)
                    added = beta_round(vector, beta_send(vector, planned, [])[0], planned, [], None, with_dot)
                    done = [a + b for a, b in zip(done, added)]
                return done

            return lax.cond(too_many, more, lambda done: done, done)

        received, token = beta_send(start_vector, first_plan, [])
        prepared = prepare(alpha_hamiltonian, alpha_pairs, pair_tables, [])
        common = (prepared, cross_pairs, cross_signs, device)
        width = wide + narrow
        columns = arrived.reshape(n_alpha * rows, wide)
        first = alpha_sum([columns], *common, 0, token[0], WORK, width, 0, [])
        (total,) = alpha_sum(arrived_few, *common, border // SB, [], 0, width, wide, first)
        returned = turn(total.reshape(n_alpha, rows, width))
        dots = [jnp.sum(columns * total[:, :wide], axis=0, keepdims=True)]
        last = total[:, wide:].reshape(n_alpha, rows, narrow)
        few = [lax.dynamic_index_in_dim(last, device[0] ^ k, 0, keepdims=False) for k in range(n_alpha)]
        dots.append(sum(jnp.sum(a * b, axis=0, keepdims=True) for a, b in zip(arrived_few, few)))
        beta_term, sums = beta_side(start_vector, received, [], dots, True)
        for other in to_partners([sums] * (n_beta - 1)):
            sums = sums + other
        sums = sums + lax.ppermute(sums, "alpha", [(i, i ^ 1) for i in range(n_alpha)])
        all_sums = [sums]
        for k in range(1, chips):
            pairs = [(i, ((i // 2 + k) % chips) * 2 + i % 2) for i in range(n_alpha)]
            all_sums.append(lax.ppermute(sums, "alpha", pairs))

        extra = (all_sums, start_vector, precondition)
        correction, (parts,) = correct(returned, beta_term, device, wide, narrow, extra, [])
        arrived = turn(parts)
        correction, few = correct(returned, beta_term, device, wide, narrow, extra, [correction])
        arrived_few = swap(few)
        received, token = beta_send(correction, first_plan, [])
        columns = arrived.reshape(n_alpha * rows, wide)
        (total,) = alpha_sum([columns], *common, 0, token[0], WORK, wide, 0, [])
        returned = turn(total.reshape(n_alpha, rows, wide))
        totals = alpha_sum(arrived_few, *common, border // SB, [total, *token[1]], 10 * WORK, 0, 0, [])
        returned_few = swap(totals)
        (beta_term,) = beta_side(correction, received, totals[:1], work=WORK)
        sigma_next, _ = finish(returned, beta_term, device, 0, None, None, WORK)
        sigma_next, _ = finish(returned_few, beta_term, device, border, sigma_next)
        return correction, sigma_next

    return local


def solution(mesh):
    placed = (
        P("alpha", "beta"),
        P("alpha", "beta"),
        P(),
        P(),
        P(),
        P("beta", None),
        P("beta", None),
        P("beta", None),
        P(None, "beta"),
        P(None, "beta"),
    )
    return jax.shard_map(
        make_local(mesh.shape["alpha"], mesh.shape["beta"]),
        mesh=mesh,
        in_specs=placed,
        out_specs=(P("alpha", "beta"), P("alpha", "beta")),
        check_vma=False,
    )
```

```python
import jax
import jax.numpy as jnp
from jax import lax
from jax.experimental import pallas as pl
from jax.experimental.pallas import tpu as pltpu
from jax.sharding import PartitionSpec as P

SB = 128
SHARE = 0.375
WORK = 20_000_000_000
VMEM_BYTES = 60 * 1024 * 1024
f32 = jnp.float32
bf16 = jnp.bfloat16


def params():
    return pltpu.CompilerParams(vmem_limit_bytes=VMEM_BYTES)


def divisor(number, most):
    return max(d for d in range(1, most + 1) if number % d == 0)


def halves(x):
    high = x.astype(bf16)
    return high, (x - high.astype(f32)).astype(bf16)


def mul(a, b):
    return jnp.dot(a, b, preferred_element_type=f32)


def cost(flops, count):
    return pl.CostEstimate(flops=max(flops, 1), bytes_accessed=max(count, 1), transcendentals=0)


def prepare(alpha_hamiltonian, alpha_pairs, pair_tables, after):
    size = alpha_hamiltonian.shape[0]
    nq = alpha_pairs.shape[0]
    depth = (nq + 1) * size
    npair = pair_tables.shape[0]

    def kernel(h_ref, p_ref, t_ref, *refs):
        a_high, a_low, t_high, t_low = refs[-4:]
        for q in range(nq + 1):
            high, low = halves(h_ref[...] if q == 0 else p_ref[q - 1])
            a_high[:, q * size : (q + 1) * size] = high
            a_low[:, q * size : (q + 1) * size] = low
        for p in range(npair):
            high, low = halves(t_ref[p])
            t_high[p, :SB, :] = high
            t_high[p, SB:, :] = high
            t_low[p] = low

    shapes = [(size, depth), (size, depth), (npair, 2 * SB, SB), (npair, SB, SB)]
    return pl.pallas_call(
        kernel,
        in_specs=[pl.BlockSpec(memory_space=pltpu.VMEM)] * 3 + [pl.BlockSpec(memory_space=pl.ANY)] * len(after),
        out_specs=[pl.BlockSpec(memory_space=pltpu.VMEM)] * 4,
        out_shape=[jax.ShapeDtypeStruct(shape, bf16) for shape in shapes],
        compiler_params=params(),
        cost_estimate=cost(0, 0),
        name="prepare",
    )(alpha_hamiltonian, alpha_pairs, pair_tables, *after)


def pack(vector, device, parts, start, width, listed, after):
    rows = vector.shape[0]

    def kernel(device_ref, source, *refs):
        targets = refs[len(after) : -2]
        held, sems = refs[-2:]
        taken = []
        given = []
        for j in range(parts):
            at = pl.multiple_of(start + ((device_ref[0] ^ j) if listed else j) * width, SB)
            target = targets[j] if listed else targets[0].at[j]
            taken.append(pltpu.make_async_copy(source.at[:, pl.ds(at, width)], held.at[j], sems.at[0, j]))
            given.append(pltpu.make_async_copy(held.at[j], target, sems.at[1, j]))
        for copy in taken:
            copy.start()
        for first, second in zip(taken, given):
            first.wait()
            second.start()
        for copy in given:
            copy.wait()

    anywhere = pl.BlockSpec(memory_space=pl.ANY)
    shapes = [(rows, width)] * parts if listed else [(parts, rows, width)]
    return pl.pallas_call(
        kernel,
        in_specs=[pl.BlockSpec(memory_space=pltpu.SMEM)] + [anywhere] * (1 + len(after)),
        out_specs=[anywhere] * len(shapes),
        out_shape=[jax.ShapeDtypeStruct(shape, f32) for shape in shapes],
        scratch_shapes=[pltpu.VMEM((parts, rows, width), f32), pltpu.SemaphoreType.DMA((2, parts))],
        compiler_params=params(),
        cost_estimate=cost(0, 0),
        name="pack",
    )(device, vector, *after)


def alpha_sum(columns, prepared, cross_pairs, cross_signs, device, start, after, work, full, offset, previous):
    size, width = prepared[1].shape[0], columns[0].shape[1]
    count = len(columns)
    rows = size // count
    depth = prepared[1].shape[1]
    nq = cross_pairs.shape[0]
    blocks = width // SB
    per = divisor(blocks, 9)
    steps = blocks // per
    wide = per * SB

    def kernel(device_ref, pairs_ref, signs_ref, *refs):
        v_any = refs[:count]
        prepared_any = refs[count : count + 4]
        outs = refs[count + 4 + len(after) + len(previous) :][: 1 if full else count]
        v_held, out_held, a_high, a_low, t_high, t_low, even, odd, sems, once = refs[-10:]

        def at(g):
            return pl.ds(pl.multiple_of(g * wide, SB), wide)

        def row(k):
            return pl.ds(pl.multiple_of((device_ref[0] ^ k) * rows, rows) if count > 1 else 0, rows)

        class Several:
            def __init__(self, copies):
                self.copies = copies

            def start(self):
                for copy in self.copies:
                    copy.start()

            def wait(self):
                for copy in self.copies:
                    copy.wait()

        def taken(g):
            return Several(
                [
                    pltpu.make_async_copy(v_any[k].at[:, at(g)], v_held.at[g, row(k)], sems.at[0, g, k])
                    for k in range(count)
                ]
            )

        def given(g):
            if full:
                to = pl.ds(offset + g * wide, wide)
                return pltpu.make_async_copy(out_held.at[g], outs[0].at[:, to], sems.at[1, g, 0])
            return Several(
                [
                    pltpu.make_async_copy(out_held.at[g, row(k)], outs[k].at[:, at(g)], sems.at[1, g, k])
                    for k in range(count)
                ]
            )

        held = (a_high, a_low, t_high, t_low)
        loads = [pltpu.make_async_copy(prepared_any[i], held[i], once.at[i]) for i in range(4)]
        for load in loads[2:]:
            load.start()
        taken(0).start()
        for load in loads[:2]:
            load.start()
        for g in range(1, steps):
            taken(g).start()
        for load in loads[2:]:
            load.wait()

        def build(g, b):
            high, low = halves(v_held[g])
            b[:size, :] = high
            b[depth : depth + size, :] = low
            first = start + device_ref[0] * blocks + g * per
            for t in range(per):
                here = slice(t * SB, (t + 1) * SB)
                both = jnp.concatenate([high[:, here], low[:, here]], axis=1)
                chosen = [pairs_ref[q, first + t] for q in range(nq)]
                x = mul(both, jnp.concatenate([t_high[p] for p in chosen], axis=1))
                x = x + mul(high[:, here], jnp.concatenate([t_low[p] for p in chosen], axis=1))
                for q in range(nq):
                    x_high, x_low = halves(x[:, q * SB : (q + 1) * SB] * signs_ref[q, first + t].astype(f32))
                    row = (q + 1) * size
                    b[row : row + size, here] = x_high
                    b[depth + row : depth + row + size, here] = x_low

        taken(0).wait()
        build(0, even)
        for load in loads[:2]:
            load.wait()
        for g in range(steps):
            b, other = (even, odd) if g % 2 == 0 else (odd, even)
            if g + 1 < steps:
                taken(g + 1).wait()
                build(g + 1, other)
            out_held[g] = mul(a_high[...], b[:depth, :]) + mul(a_high[...], b[depth:, :]) + mul(a_low[...], b[:depth, :])
            given(g).start()
        for g in range(steps):
            given(g).wait()

    anywhere = pl.BlockSpec(memory_space=pl.ANY)
    return pl.pallas_call(
        kernel,
        in_specs=[pl.BlockSpec(memory_space=pltpu.SMEM)] * 3 + [anywhere] * (count + 4 + len(after) + len(previous)),
        out_specs=[anywhere] * (1 if full else count),
        out_shape=[jax.ShapeDtypeStruct((size, full), f32)]
        if full
        else [jax.ShapeDtypeStruct((rows, width), f32)] * count,
        input_output_aliases={3 + count + 4 + len(after): 0} if previous else {},
        scratch_shapes=[pltpu.VMEM((steps, size, wide), f32)] * 2
        + [pltpu.VMEM(a.shape, bf16) for a in prepared]
        + [
            pltpu.VMEM((2 * depth, wide), bf16),
            pltpu.VMEM((2 * depth, wide), bf16),
            pltpu.SemaphoreType.DMA((2, steps, count)),
            pltpu.SemaphoreType.DMA((4,)),
        ],
        compiler_params=params(),
        cost_estimate=cost(work, work // 300),
        name="alpha_sum",
    )(device, cross_pairs, cross_signs, *columns, *prepared, *after, *previous)


def earlier(lanes):
    row = lax.broadcasted_iota(jnp.int32, (lanes, lanes), 0)
    column = lax.broadcasted_iota(jnp.int32, (lanes, lanes), 1)
    return jnp.where(row < column, 1.0, 0.0).astype(bf16)


def mark(source_blocks, me, parts, after):
    blocks, kb = source_blocks.shape
    lanes = -(-blocks // SB) * SB
    tall = -(-parts // 8) * 8

    def kernel(me_ref, source_ref, *refs):
        marks_refs = refs[len(after) : len(after) + parts - 1]
        found_ref, held = refs[-2:]
        lane = lax.broadcasted_iota(jnp.int32, (blocks, lanes), 1)

        def hit(s, k):
            return (source_ref[:, k : k + 1] - s * blocks == lane) & (lane < blocks)

        held[...] = jnp.zeros_like(held)
        worst = jnp.zeros((1, 1), f32)
        for s in range(parts):
            needed = jnp.zeros((1, lanes), f32)
            for k in range(kb):
                needed = jnp.maximum(needed, jnp.max(jnp.where(hit(s, k), 1.0, 0.0), axis=0, keepdims=True))
            held[s : s + 1, :] = needed
            count = jnp.sum(needed, axis=1, keepdims=True)
            worst = jnp.maximum(worst, jnp.where(me_ref[0] == s, 0.0, count))
        place = mul(held[...].astype(bf16), earlier(lanes))
        for k in range(kb):
            found = jnp.zeros((blocks, 1), f32)
            for s in range(parts):
                found = found + jnp.sum(jnp.where(hit(s, k), place[s : s + 1, :], 0.0), axis=1, keepdims=True)
            found_ref[:, k : k + 1] = found.astype(jnp.int32)
        for k, marks_ref in enumerate(marks_refs, 1):
            marks_ref[...] = jnp.zeros_like(marks_ref)
            marks_ref[0:1, :] = held[pl.ds(me_ref[0] ^ k, 1), :]
            marks_ref[1:2, :] = jnp.broadcast_to(worst, (1, lanes))

    return pl.pallas_call(
        kernel,
        in_specs=[pl.BlockSpec(memory_space=pltpu.SMEM), pl.BlockSpec(memory_space=pltpu.VMEM)]
        + [pl.BlockSpec(memory_space=pl.ANY)] * len(after),
        out_specs=[pl.BlockSpec(memory_space=pltpu.VMEM)] * parts,
        out_shape=[jax.ShapeDtypeStruct((8, lanes), f32)] * (parts - 1)
        + [jax.ShapeDtypeStruct((blocks, kb), jnp.int32)],
        scratch_shapes=[pltpu.VMEM((tall, lanes), f32)],
        compiler_params=params(),
        cost_estimate=cost(0, 0),
        name="mark",
    )(me, source_blocks, *after)


def positions(marks, first, cap):
    lanes = marks[0].shape[1]
    count = len(marks)
    tall = -(-count // 8) * 8

    def kernel(*refs):
        out_ref, held = refs[-2:]
        held[...] = jnp.zeros_like(held)
        for k in range(count):
            held[k : k + 1, :] = refs[k][0:1, :]
        needed = held[...]
        slot = mul(needed.astype(bf16), earlier(lanes)).astype(jnp.int32) - first
        out_ref[...] = jnp.where((needed > 0) & (slot >= 0) & (slot < cap), slot, cap)

    return pl.pallas_call(
        kernel,
        in_specs=[pl.BlockSpec(memory_space=pltpu.VMEM)] * count,
        out_specs=pl.BlockSpec(memory_space=pltpu.VMEM),
        out_shape=jax.ShapeDtypeStruct((tall, lanes), jnp.int32),
        scratch_shapes=[pltpu.VMEM((tall, lanes), f32)],
        compiler_params=params(),
        cost_estimate=cost(0, 0),
        name="positions",
    )(*marks)


def gather_blocks(vector, slots, count, cap, after):
    rows, cols = vector.shape

    def kernel(slots_ref, v_ref, *refs):
        outs = refs[len(after) :]

        @pl.loop(0, cols // SB, unroll=4)
        def _(b):
            block = v_ref[:, pl.ds(pl.multiple_of(b * SB, SB), SB)]
            for k in range(count):
                outs[k][slots_ref[k, b]] = block

    shape = (cap + 1, rows, SB)
    return pl.pallas_call(
        kernel,
        grid_spec=pltpu.PrefetchScalarGridSpec(
            num_scalar_prefetch=1,
            grid=(1,),
            in_specs=[pl.BlockSpec(vector.shape, lambda g, *_: (0, 0))]
            + [pl.BlockSpec(memory_space=pl.ANY)] * len(after),
            out_specs=[pl.BlockSpec(shape, lambda g, *_: (0, 0, 0))] * count,
        ),
        out_shape=[jax.ShapeDtypeStruct(shape, f32)] * count,
        compiler_params=params(),
        cost_estimate=cost(0, 0),
        name="gather_blocks",
    )(slots, vector, *after)


def beta_sum(vector, received, slots, signs, pair_index, pair_tables, after, dots=None, with_dot=False, work=0):
    rows, cols = vector.shape
    blocks = cols // SB
    npair = pair_tables.shape[0]
    kb = slots.shape[0]
    far = len(received)
    each = received[0].shape[0]
    dots = [] if dots is None else dots
    per = divisor(blocks, 16)
    steps = blocks // per

    def kernel(slots_ref, sign_ref, pair_ref, *refs):
        v_ref, t_ref = refs[:2]
        r_refs = refs[2 : 2 + far]
        at = 2 + far + len(after)
        dot_refs = refs[at : at + len(dots)]
        out_ref = refs[at + len(dots)]
        pool, wide, t_high, t_low, sems = refs[-5:]
        g = pl.program_id(0)

        @pl.when(g == 0)
        def _():
            copies = [
                pltpu.make_async_copy(r_refs[i], pool.at[pl.ds(i * each, each)], sems.at[i]) for i in range(far)
            ]
            for copy in copies:
                copy.start()
            for p in range(npair):
                high, low = halves(t_ref[p])
                t_high[p * SB : (p + 1) * SB, :] = high
                t_low[p * SB : (p + 1) * SB, :] = low
            for copy in copies:
                copy.wait()

        wide[...] = jnp.zeros_like(wide)
        for t in range(per):
            target = g * per + t
            for k in range(kb):
                slot = slots_ref[k, target]
                own = v_ref[:, pl.ds(pl.multiple_of(lax.min(slot, blocks - 1) * SB, SB), SB)]
                other = pool[lax.max(slot - blocks, 0)]
                block = jnp.where(slot < blocks, own, other) * sign_ref[k, target].astype(f32)
                at = pl.ds(pl.multiple_of(pair_ref[k, target] * SB, SB), SB)
                wide[t * rows : (t + 1) * rows, at] += block
        high, low = halves(wide[...])
        total = mul(high, t_high[...]) + mul(low, t_high[...]) + mul(high, t_low[...])
        for t in range(per):
            out_ref[:, t * SB : (t + 1) * SB] = total[t * rows : (t + 1) * rows]
        if with_dot:
            sums_ref = refs[-6]
            dot = jnp.zeros((rows, SB), f32)
            square = jnp.zeros((rows, SB), f32)
            for t in range(per):
                v = v_ref[:, pl.ds(pl.multiple_of((g * per + t) * SB, SB), SB)]
                dot = dot + total[t * rows : (t + 1) * rows] * v
                square = square + v * v
            dot = jnp.sum(dot, axis=0, keepdims=True)
            square = jnp.sum(square, axis=0, keepdims=True)

            @pl.when(g == 0)
            def _():
                sums_ref[...] = jnp.zeros_like(sums_ref)

            sums_ref[0:1, :] += dot
            if dots:
                sums_ref[1:2, :] += square

            @pl.when(g == steps - 1)
            def _():
                value = sums_ref[...]
                for ref in dot_refs:
                    for at in range(0, ref.shape[1], SB):
                        first = lax.broadcasted_iota(jnp.int32, value.shape, 0) == 0
                        value = value + jnp.where(first, ref[:, at : at + SB], 0.0)
                sums_ref[...] = value

    out = pl.pallas_call(
        kernel,
        grid_spec=pltpu.PrefetchScalarGridSpec(
            num_scalar_prefetch=3,
            grid=(steps,),
            in_specs=[
                pl.BlockSpec((rows, cols), lambda g, *_: (0, 0)),
                pl.BlockSpec(pair_tables.shape, lambda g, *_: (0, 0, 0)),
            ]
            + [pl.BlockSpec(memory_space=pl.ANY)] * (far + len(after))
            + [pl.BlockSpec(dot.shape, lambda g, *_: (0, 0)) for dot in dots],
            out_specs=[pl.BlockSpec((rows, per * SB), lambda g, *_: (0, g))]
            + ([pl.BlockSpec((8, SB), lambda g, *_: (0, 0))] if with_dot else []),
            scratch_shapes=[
                pltpu.VMEM((far * each, rows, SB), f32),
                pltpu.VMEM((per * rows, npair * SB), f32),
                pltpu.VMEM((npair * SB, SB), bf16),
                pltpu.VMEM((npair * SB, SB), bf16),
                pltpu.SemaphoreType.DMA((far,)),
            ],
        ),
        out_shape=[jax.ShapeDtypeStruct((rows, cols), f32)]
        + ([jax.ShapeDtypeStruct((8, SB), f32)] if with_dot else []),
        compiler_params=params(),
        cost_estimate=cost(work, work // 300),
        name="beta_sum",
    )(slots, signs, pair_index, vector, pair_tables, *received, *after, *dots)
    return list(out)


def correct(returned, beta_term, device, wide, narrow, extra, previous):
    rows, cols = beta_term.shape
    parts = returned.shape[0]
    sums = [] if extra is None else extra[0]
    wholes = [beta_term] + ([] if extra is None else [extra[1], extra[2]])
    count = len(wholes)
    sent = parts if previous else 1

    def kernel(device_ref, *refs):
        sum_refs = refs[: len(sums)]
        whole_refs = refs[len(sums) :][:count]
        part_ref = refs[len(sums) + count]
        out_refs = refs[len(sums) + count + 1 + len(previous) :][: 1 + sent]
        held, sems, out_sems = refs[-3:]
        pieces = []
        for j in range(parts):
            if previous:
                place = device_ref[0] ^ j
                at = pl.multiple_of(parts * wide + place * narrow, SB)
                pieces.append((held, j, at, part_ref.at[place, :, wide:], out_refs[1 + j]))
            else:
                pieces.append((held, j, j * wide, part_ref.at[j, :, :wide], out_refs[1].at[j]))
        taken = []
        given = []
        for p, (buffer, j, start, part, target) in enumerate(pieces):
            at = pl.ds(start, buffer.shape[-1])
            taken.append(
                [pltpu.make_async_copy(whole_refs[i].at[:, at], buffer.at[i, j], sems.at[i, p]) for i in range(count)]
                + [pltpu.make_async_copy(part, buffer.at[count, j], sems.at[count, p])]
            )
            given.append([pltpu.make_async_copy(buffer.at[count, j], out_refs[0].at[:, at], out_sems.at[0, p])])
            given[-1].append(pltpu.make_async_copy(buffer.at[count, j], target, out_sems.at[1, p]))
        for copies in taken:
            for copy in copies:
                copy.start()
        if extra is not None:
            total = sum_refs[0][...]
            for ref in sum_refs[1:]:
                total = total + ref[...]
            both = [jnp.sum(total[i : i + 1], axis=1, keepdims=True) for i in range(2)]
            theta = both[0] / both[1]
        for p, (buffer, j, _, _, _) in enumerate(pieces):
            for copy in taken[p]:
                copy.wait()
            value = buffer[0, j] + buffer[count, j]
            if extra is not None:
                value = (value - theta * buffer[1, j]) / buffer[2, j]
            buffer[count, j] = value
            for copy in given[p]:
                copy.start()
        for copies in given:
            for copy in copies:
                copy.wait()

    anywhere = pl.BlockSpec(memory_space=pl.ANY)
    shapes = [(rows, cols)] + ([(rows, narrow)] * parts if previous else [(parts, rows, wide)])
    out = pl.pallas_call(
        kernel,
        in_specs=[pl.BlockSpec(memory_space=pltpu.SMEM)]
        + [pl.BlockSpec(memory_space=pltpu.VMEM)] * len(sums)
        + [anywhere] * (count + 1 + len(previous)),
        out_specs=[anywhere] * (1 + sent),
        out_shape=[jax.ShapeDtypeStruct(shape, f32) for shape in shapes],
        input_output_aliases={1 + len(sums) + count + 1: 0} if previous else {},
        scratch_shapes=[
            pltpu.VMEM((count + 1, parts, rows, narrow if previous else wide), f32),
            pltpu.SemaphoreType.DMA((count + 1, parts)),
            pltpu.SemaphoreType.DMA((2, parts)),
        ],
        compiler_params=params(),
        cost_estimate=cost(0, 0),
        name="correct",
    )(device, *sums, *wholes, returned, *previous)
    return out[0], out[1:]


def finish(returned, beta_term, device, start, previous, extra=None, work=0):
    rows, cols = beta_term.shape
    listed = isinstance(returned, (list, tuple))
    arrays = list(returned) if listed else [returned]
    parts = len(arrays) if listed else returned.shape[0]
    width = arrays[0].shape[-1]
    sums = [] if extra is None else extra[0]
    wholes = [beta_term] + ([] if extra is None else [extra[1], extra[2]])
    count = len(wholes)
    aliased = [] if previous is None else [previous]
    sent = [] if extra is None else arrays

    def kernel(device_ref, *refs):
        sum_refs = refs[: len(sums)]
        whole_refs = refs[len(sums) :][:count]
        part_refs = refs[len(sums) + count :][: len(arrays)]
        out_refs = refs[len(sums) + count + len(arrays) + len(aliased) :][: 1 + len(sent)]
        held, sems, out_sems = refs[-3:]

        def piece(among, j):
            return among[j] if listed else among[0].at[j]

        taken = []
        given = []
        for j in range(parts):
            place = device_ref[0] ^ j if listed else j
            at = pl.ds(pl.multiple_of(start + place * width, SB), width)
            taken.append(
                [pltpu.make_async_copy(whole_refs[i].at[:, at], held.at[i, j], sems.at[i, j]) for i in range(count)]
                + [pltpu.make_async_copy(piece(part_refs, j), held.at[count, j], sems.at[count, j])]
            )
            given.append([pltpu.make_async_copy(held.at[count, j], out_refs[0].at[:, at], out_sems.at[0, j])])
            if sent:
                target = piece(out_refs[1:], j)
                given[-1].append(pltpu.make_async_copy(held.at[count, j], target, out_sems.at[1, j]))
        for copies in taken:
            for copy in copies:
                copy.start()
        if extra is not None:
            total = sum_refs[0][...]
            for ref in sum_refs[1:]:
                total = total + ref[...]
            both = [jnp.sum(total[i : i + 1], axis=1, keepdims=True) for i in range(2)]
            theta = both[0] / both[1]
        for j in range(parts):
            for copy in taken[j]:
                copy.wait()
            value = held[0, j] + held[count, j]
            if extra is not None:
                value = (value - theta * held[1, j]) / held[2, j]
            held[count, j] = value
            for copy in given[j]:
                copy.start()
        for copies in given:
            for copy in copies:
                copy.wait()

    anywhere = pl.BlockSpec(memory_space=pl.ANY)
    out = pl.pallas_call(
        kernel,
        in_specs=[pl.BlockSpec(memory_space=pltpu.SMEM)]
        + [pl.BlockSpec(memory_space=pltpu.VMEM)] * len(sums)
        + [anywhere] * (count + len(arrays) + len(aliased)),
        out_specs=[anywhere] * (1 + len(sent)),
        out_shape=[jax.ShapeDtypeStruct(a.shape, f32) for a in [beta_term] + sent],
        input_output_aliases={1 + len(sums) + count + len(arrays): 0} if aliased else {},
        scratch_shapes=[
            pltpu.VMEM((count + 1, parts, rows, width), f32),
            pltpu.SemaphoreType.DMA((count + 1, parts)),
            pltpu.SemaphoreType.DMA((2, parts)),
        ],
        compiler_params=params(),
        cost_estimate=cost(work, work // 300),
        name="finish" if extra is None else "correct",
    )(device, *sums, *wholes, *arrays, *aliased)
    return out[0], out[1:]


def make_local(n_alpha, n_beta):
    chips = n_alpha // 2

    def to_partners(parts):
        return [lax.ppermute(part, "beta", [(i, i ^ k) for i in range(n_beta)]) for k, part in enumerate(parts, 1)]

    def turn(parts):
        return lax.all_to_all(parts, "alpha", 0, 0, tiled=True)

    def swap(parts):
        moved = list(parts)
        for k in range(n_alpha - 1, 0, -1):
            moved[k] = lax.ppermute(parts[k], "alpha", [(i, i ^ k) for i in range(n_alpha)])
        return moved

    def local(
        start_vector,
        precondition,
        alpha_hamiltonian,
        alpha_pairs,
        pair_tables,
        source_blocks,
        pair_index,
        phase_signs,
        cross_pairs,
        cross_signs,
    ):
        rows, cols = start_vector.shape
        blocks = cols // SB
        mine = blocks // n_alpha
        few = max(1, round(mine * SHARE))
        wide, narrow = (mine - few) * SB, few * SB
        border = n_alpha * wide
        cap = (blocks + 1) // 2
        device = lax.axis_index("alpha").astype(jnp.int32).reshape(1)
        me = lax.axis_index("beta").astype(jnp.int32)

        (sent,) = pack(start_vector, device, n_alpha, 0, wide, False, [])
        arrived = turn(sent)
        sent_few = pack(start_vector, device, n_alpha, border, narrow, True, [sent])
        arrived_few = swap(sent_few)

        *marks, found = mark(source_blocks, me.reshape(1), n_beta, [sent])
        worst = marks[0][1:2, :1]
        marks = to_partners(marks)
        for other in marks:
            worst = jnp.maximum(worst, other[1:2, :1])
        too_many = worst[0, 0] > cap
        pairs_by_k = pair_index.T

        def plan(r):
            partner = (source_blocks // blocks) ^ me
            here = (found >= r * cap) & (found < (r + 1) * cap) & (partner != 0)
            far_slot = blocks + (partner - 1) * (cap + 1) + found - r * cap
            mine = (partner == 0) & (r == 0)
            slots = jnp.where(mine, source_blocks - me * blocks, jnp.where(here, far_slot, 0))
            signs = jnp.where(mine | here, phase_signs, 0)
            return positions(marks, r * cap, cap), slots.T, signs.T

        first_plan = plan(0)

        def beta_send(vector, planned, after):
            sent = gather_blocks(vector, planned[0], n_beta - 1, cap, after)
            received = to_partners(sent)
            return received, (received[:2], received[2:])

        def beta_round(vector, received, planned, after, dots=None, with_dot=False, work=0):
            _, slots, signs = planned
            return beta_sum(vector, received, slots, signs, pairs_by_k, pair_tables, after, dots, with_dot, work)

        def beta_side(vector, received, after, dots=None, with_dot=False, work=0):
            done = beta_round(vector, received, first_plan, after, dots, with_dot, work)

            def more(done):
                for r in range(1, -(-blocks // cap)):
                    planned = plan(r)
                    added = beta_round(vector, beta_send(vector, planned, [])[0], planned, [], None, with_dot)
                    done = [a + b for a, b in zip(done, added)]
                return done

            return lax.cond(too_many, more, lambda done: done, done)

        received, token = beta_send(start_vector, first_plan, [])
        prepared = prepare(alpha_hamiltonian, alpha_pairs, pair_tables, [])
        common = (prepared, cross_pairs, cross_signs, device)
        width = wide + narrow
        columns = arrived.reshape(n_alpha * rows, wide)
        first = alpha_sum([columns], *common, 0, token[0], WORK, width, 0, [])
        (total,) = alpha_sum(arrived_few, *common, border // SB, [], 0, width, wide, first)
        returned = turn(total.reshape(n_alpha, rows, width))
        dots = [jnp.sum(columns * total[:, :wide], axis=0, keepdims=True)]
        last = total[:, wide:].reshape(n_alpha, rows, narrow)
        few = [lax.dynamic_index_in_dim(last, device[0] ^ k, 0, keepdims=False) for k in range(n_alpha)]
        dots.append(sum(jnp.sum(a * b, axis=0, keepdims=True) for a, b in zip(arrived_few, few)))
        beta_term, sums = beta_side(start_vector, received, [], dots, True)
        for other in to_partners([sums] * (n_beta - 1)):
            sums = sums + other
        sums = sums + lax.ppermute(sums, "alpha", [(i, i ^ 1) for i in range(n_alpha)])
        all_sums = [sums]
        for k in range(1, chips):
            pairs = [(i, ((i // 2 + k) % chips) * 2 + i % 2) for i in range(n_alpha)]
            all_sums.append(lax.ppermute(sums, "alpha", pairs))

        extra = (all_sums, start_vector, precondition)
        correction, (parts,) = correct(returned, beta_term, device, wide, narrow, extra, [])
        arrived = turn(parts)
        correction, few = correct(returned, beta_term, device, wide, narrow, extra, [correction])
        arrived_few = swap(few)
        received, token = beta_send(correction, first_plan, [])
        columns = arrived.reshape(n_alpha * rows, wide)
        (total,) = alpha_sum([columns], *common, 0, token[0], WORK, wide, 0, [])
        returned = turn(total.reshape(n_alpha, rows, wide))
        totals = alpha_sum(arrived_few, *common, border // SB, [total, *token[1]], 10 * WORK, 0, 0, [])
        returned_few = swap(totals)
        (beta_term,) = beta_side(correction, received, totals[:1], work=WORK)
        sigma_next, _ = finish(returned, beta_term, device, 0, None, None, WORK)
        sigma_next, _ = finish(returned_few, beta_term, device, border, sigma_next)
        return correction, sigma_next

    return local


def solution(mesh):
    placed = (
        P("alpha", "beta"),
        P("alpha", "beta"),
        P(),
        P(),
        P(),
        P("beta", None),
        P("beta", None),
        P("beta", None),
        P(None, "beta"),
        P(None, "beta"),
    )
    return jax.shard_map(
        make_local(mesh.shape["alpha"], mesh.shape["beta"]),
        mesh=mesh,
        in_specs=placed,
        out_specs=(P("alpha", "beta"), P("alpha", "beta")),
        check_vma=False,
    )
```
